256 devices in a mesh: blk: 32 (over z, y_lo, core), head: 8 (over x, y_hi).
Axes of the slice: x: 4, y: 4 (y_hi: 2, y_lo: 2; y = y_hi * 2 + y_lo), z: 8, core: 2. Of those that a mesh axis runs over, the one named last changes fastest.
Arguments:
- queries: bfloat16 [2048, 16384], P('blk', 'head'), may hold values from -128 to 128
- keys: bfloat16 [16384, 1024], P('blk', 'head'), may hold values from -6 to 6
- values: bfloat16 [16384, 1024], P('blk', 'head'), may hold values from -6 to 6
- out_weight: bfloat16 [16384, 16384], P('head', 'blk'), may hold values from -0.046875 to 0.046875
- cache_len: int32 [1], replicated, may hold values from 8192 to 14336
- block_order: int32 [32], P('blk'), may hold values from 0 to 31, each once
Outputs:
- projected: bfloat16 [2048, 16384], P('head', 'blk')
The draws below stay inside these ranges and needn't reach their ends.
Inputs may be any that keep to these rules, and one draw needn't show every extreme that they name: `block_order`: a permutation of the query blocks.
All inputs are finite; a program needn't handle non-finite values.
Results may differ from the reference program's by a relative error of at most 0.017.
Values may be sent and summed in bfloat16 or wider, within the bound.
No kernel may reach another device: no remote copies, remote signals or barrier semaphores. Data moves between devices by JAX's collectives and lax.ppermute only.
A program may use at most 128 MiB of HBM per device.

```python
import jax
import jax.numpy as jnp
from jax import lax

D = 16384
QUERY_HEADS = 128
KEY_VALUE_HEADS = 8
HEAD_SIZE = 128
Q_DEV = 64
C_DEV = 512
TURN_TOKENS = 2048
CACHE_POSITIONS = 16384
N_BLK = 32


def common_keys(key):
    return jnp.clip(jax.random.normal(key, (CACHE_POSITIONS, KEY_VALUE_HEADS * HEAD_SIZE), jnp.float32), -5.0, 5.0)


def draw_keys(key, part):
    base = common_keys(key)
    return base.astype(jnp.bfloat16)


def draw_queries(key, part):
    key = jax.random.fold_in(key, 5)
    normal_part = jax.random.fold_in(key, 0)
    result = 2.5 * jnp.clip(jax.random.normal(normal_part, (TURN_TOKENS, QUERY_HEADS * HEAD_SIZE), jnp.float32), -5.0, 5.0)
    return result.astype(jnp.bfloat16)


def steps_of(rng, shape, cuts, low, largest):
    factor_of, own = 1.0, jax.random.fold_in(rng, 6)
    for dim, blocks in cuts:
        steps = jnp.exp(jax.random.uniform(jax.random.fold_in(own, dim), (blocks,), jnp.float32, low / len(cuts), largest / len(cuts)))
        factor_of = factor_of * jnp.repeat(steps, shape[dim] // blocks).reshape([-1 if axis == dim else 1 for axis in range(len(shape))])
    return factor_of


def scatter_about(rng, shape, scale, limit, cuts=(), held_as=jnp.bfloat16):
    array = jax.random.normal(rng, shape, jnp.float32) * scale
    if len(cuts) > 0:
        array = steps_of(rng, shape, cuts, -0.22, 0.18) * array
    return jnp.clip(array, min=-limit, max=limit).astype(held_as)


def setup_inputs(seed: int = 0) -> dict:
    streams_of = jax.random.split(jax.random.key(seed), 7)
    queries = draw_queries(jax.random.fold_in(streams_of[6], 71), 0)
    keys = draw_keys(jax.random.fold_in(streams_of[6], 71), 0)
    values = scatter_about(streams_of[2], (CACHE_POSITIONS, KEY_VALUE_HEADS * HEAD_SIZE), 1.0, 6.0, ((0, 32), (1, 8)))
    out_weight = scatter_about(streams_of[3], (QUERY_HEADS * HEAD_SIZE, D), (QUERY_HEADS * HEAD_SIZE) ** -0.5, 0.046875, ((0, 8), (1, 32)))
    cache_len = jax.random.randint(streams_of[4], (1,), CACHE_POSITIONS // 2, CACHE_POSITIONS - TURN_TOKENS + 1).astype(jnp.int32)
    block_order = jax.random.permutation(streams_of[5], N_BLK).astype(jnp.int32)
    return dict(queries=queries, keys=keys, values=values, out_weight=out_weight, cache_len=cache_len, block_order=block_order)


def combine(out_a, lse_a, out_b, lse_b):
    maxima = jnp.maximum(lse_a, lse_b)
    weight_a = jnp.exp(lse_a - maxima)
    weight_b = jnp.exp(lse_b - maxima)
    totals = weight_a + weight_b
    merged = (weight_a[..., None] * out_a + weight_b[..., None] * out_b) / totals[..., None]
    return merged, maxima + jnp.log(totals)


def reference(queries, keys, values, out_weight, cache_len, block_order):
    heads_per_group = QUERY_HEADS // KEY_VALUE_HEADS
    scale = float(HEAD_SIZE) ** -0.5
    rows_index = jnp.arange(TURN_TOKENS, dtype=jnp.int32)
    qpos = cache_len[0] + block_order[rows_index // Q_DEV] * Q_DEV + rows_index % Q_DEV
    heads_of_queries = queries.reshape(TURN_TOKENS, KEY_VALUE_HEADS, heads_per_group, HEAD_SIZE).transpose(1, 2, 0, 3)
    heads_of_keys = keys.reshape(CACHE_POSITIONS, KEY_VALUE_HEADS, HEAD_SIZE).transpose(1, 0, 2)
    heads_of_values = values.reshape(CACHE_POSITIONS, KEY_VALUE_HEADS, HEAD_SIZE).transpose(1, 0, 2)

    def per_head(operands):
        query_set, key_all, value_all = operands

        def absorb_shard(accum, shard_id):
            first = shard_id * C_DEV
            key_shard = lax.dynamic_slice_in_dim(key_all, first, C_DEV, 0)
            value_shard = lax.dynamic_slice_in_dim(value_all, first, C_DEV, 0)
            kpos = first + jnp.arange(C_DEV, dtype=jnp.int32)
            scores = jnp.einsum("gqd,kd->gqk", query_set.astype(jnp.float32), key_shard.astype(jnp.float32)) * scale
            visible = kpos[None, :] <= qpos[:, None]
            scores = jnp.where(visible[None], scores, jnp.float32(-1e30))
            maxima = jnp.max(scores, axis=-1)
            probs = jnp.exp(scores - maxima[..., None])
            totals = jnp.sum(probs, axis=-1)
            weights = probs.astype(jnp.bfloat16)
            partial_out = jnp.einsum("gqk,kd->gqd", weights.astype(jnp.float32), value_shard.astype(jnp.float32)) / totals[..., None]
            lse = maxima + jnp.log(totals)
            return combine(accum[0], accum[1], partial_out, lse), None

        start_out = jnp.zeros((heads_per_group, TURN_TOKENS, HEAD_SIZE), jnp.float32)
        start_lse = jnp.full((heads_per_group, TURN_TOKENS), -jnp.inf, jnp.float32)
        final, unused = lax.scan(absorb_shard, (start_out, start_lse), jnp.arange(N_BLK, dtype=jnp.int32))
        return final[0]

    attended = lax.map(per_head, (heads_of_queries, heads_of_keys, heads_of_values))
    attn = attended.transpose(2, 0, 1, 3).reshape(TURN_TOKENS, QUERY_HEADS * HEAD_SIZE).astype(jnp.bfloat16)
    return jnp.dot(attn, out_weight, preferred_element_type=jnp.float32).astype(jnp.bfloat16)
```

```python
import functools
import math

import jax
import jax.numpy as jnp
from jax import lax
from jax.experimental import pallas as pl
from jax.experimental.pallas import tpu as pltpu
from jax.sharding import PartitionSpec as P

HEAD = 128
GROUP = 16
TOK = 64
ROWS = GROUP * TOK
C_ROWS = 512
SCALE = math.log2(math.e) / math.sqrt(HEAD)
LOW = -1e30
RB = 256
NZ, NR = 8, 4
EXT = 32
MIB = 2**20
VMEM = pltpu.VMEM
SMEM = pltpu.SMEM


def z_shift(step):
    return [(z * NR + r, ((z + step) % NZ) * NR + r) for z in range(NZ) for r in range(NR)]


def swap(bit):
    return [(b, b ^ bit) for b in range(NZ * NR)]


def move(x, pairs):
    return lax.ppermute(x, "blk", pairs)


def prep_kernel(order_ref, q_ref, o_ref):
    for g in range(GROUP):
        o_ref[g * TOK : (g + 1) * TOK, :] = q_ref[:, g * HEAD : (g + 1) * HEAD]
    place = jnp.full((16, HEAD), order_ref[0], jnp.int32).astype(jnp.float32)
    o_ref[ROWS : ROWS + 16, :] = place.astype(jnp.bfloat16)


def prep(order, queries):
    return pl.pallas_call(
        prep_kernel,
        out_shape=jax.ShapeDtypeStruct((ROWS + 16, HEAD), jnp.bfloat16),
        in_specs=[pl.BlockSpec(memory_space=SMEM), pl.BlockSpec(memory_space=VMEM)],
        out_specs=pl.BlockSpec(memory_space=VMEM),
        name="prep",
    )(order, queries)


def pack(o_ref, acc, top):
    eye = lax.broadcasted_iota(jnp.int32, (HEAD, HEAD), 0) == lax.broadcasted_iota(
        jnp.int32, (HEAD, HEAD), 1
    )
    lines = []
    for r in range(0, ROWS, HEAD):
        total = acc[r : r + HEAD, HEAD:]
        o_ref[r : r + HEAD, :] = (acc[r : r + HEAD, :HEAD] / total).astype(jnp.bfloat16)
        lse = top[r : r + HEAD, :] + jnp.log2(total)
        lines.append(jnp.sum(jnp.where(eye, lse, 0.0), axis=0, keepdims=True))
    lse = jnp.concatenate(lines, axis=0)
    hi = lse.astype(jnp.bfloat16)
    rest = lse - hi.astype(jnp.float32)
    mid = rest.astype(jnp.bfloat16)
    low = (rest - mid.astype(jnp.float32)).astype(jnp.bfloat16)
    parts = [part.astype(jnp.float32) for part in (hi, mid, low)]
    tail = jnp.concatenate(parts + [jnp.zeros_like(lse)], axis=0)
    o_ref[ROWS : ROWS + EXT, :] = tail.astype(jnp.bfloat16)


def flash_kernel(sizes, first, last, pos_ref, base_ref, *refs):
    n = len(sizes)
    q_ref = refs[0]
    kv_refs = refs[1 : 1 + n]
    refs = refs[1 + n :]
    if not first:
        acc_in, top_in = refs[0], refs[1]
        refs = refs[2:]
    if last:
        out_ref, acc, top = refs
    else:
        acc, top = refs
    if first:
        acc[...] = jnp.zeros_like(acc)
        top[...] = jnp.full_like(top, LOW)
    else:
        acc[...] = acc_in[...]
        top[...] = top_in[...]
    pos = pos_ref[pl.program_id(0)]

    def absorb(kv_ref, size, base, masked):
        k = kv_ref[:, :HEAD]
        v = kv_ref[:, HEAD:]
        v1 = jnp.concatenate([v, jnp.ones_like(v)], axis=1)
        for r in range(0, ROWS, RB):
            s = lax.dot_general(
                q_ref[r : r + RB, :],
                k,
                (((1,), (1,)), ((), ())),
                preferred_element_type=jnp.float32,
            )
            s = s * SCALE
            if masked:
                row = lax.broadcasted_iota(jnp.int32, (RB, size), 0) % TOK
                col = lax.broadcasted_iota(jnp.int32, (RB, size), 1)
                s = jnp.where(base + col <= pos + row, s, LOW)
            old = top[r : r + RB, :]
            new = jnp.maximum(old, jnp.max(s, axis=1, keepdims=True))
            p = jnp.exp2(s - jnp.tile(new, (1, size // HEAD))).astype(jnp.bfloat16)
            shrink = jnp.tile(jnp.exp2(old - new), (1, 2))
            acc[r : r + RB, :] = acc[r : r + RB, :] * shrink + jnp.dot(
                p, v1, preferred_element_type=jnp.float32
            )
            top[r : r + RB, :] = new

    for j, size in enumerate(sizes):
        base = base_ref[j]

        @pl.when(base + size - 1 <= pos)
        def _():
            absorb(kv_refs[j], size, base, False)

        @pl.when((base + size - 1 > pos) & (base <= pos + TOK - 1))
        def _():
            absorb(kv_refs[j], size, base, True)

    if last:
        pack(out_ref, acc, top)


def flash(pos, bases, qs, kvs, state, last):
    n_q = qs.shape[0]
    sizes = tuple(kv.shape[0] for kv in kvs)
    first = state is None
    row = lambda width: pl.BlockSpec((None, ROWS, width), lambda i, *_: (i, 0, 0))
    state_specs = [row(2 * HEAD), row(HEAD)]
    state_shapes = [
        jax.ShapeDtypeStruct((n_q, ROWS, 2 * HEAD), jnp.float32),
        jax.ShapeDtypeStruct((n_q, ROWS, HEAD), jnp.float32),
    ]
    in_specs = [pl.BlockSpec((None, ROWS + 16, HEAD), lambda i, *_: (i, 0, 0))]
    in_specs += [pl.BlockSpec((size, 2 * HEAD), lambda i, *_: (0, 0)) for size in sizes]
    args = [qs, *kvs]
    if not first:
        in_specs += state_specs
        args += list(state)
    if last:
        out_shape = jax.ShapeDtypeStruct((n_q, ROWS + EXT, HEAD), jnp.bfloat16)
        out_specs = pl.BlockSpec((None, ROWS + EXT, HEAD), lambda i, *_: (i, 0, 0))
        scratch = [VMEM((ROWS, 2 * HEAD), jnp.float32), VMEM((ROWS, HEAD), jnp.float32)]
        aliases = {}
    else:
        out_shape, out_specs, scratch = state_shapes, state_specs, []
        aliases = {} if first else {2 + len(args) - 2: 0, 2 + len(args) - 1: 1}
    keys = sum(sizes)
    return pl.pallas_call(
        functools.partial(flash_kernel, sizes, first, last),
        out_shape=out_shape,
        grid_spec=pltpu.PrefetchScalarGridSpec(
            num_scalar_prefetch=2,
            grid=(n_q,),
            in_specs=in_specs,
            out_specs=out_specs,
            scratch_shapes=scratch,
        ),
        input_output_aliases=aliases,
        compiler_params=pltpu.CompilerParams(vmem_limit_bytes=32 * MIB),
        cost_estimate=pl.CostEstimate(
            flops=n_q * ROWS * keys * HEAD * 16, bytes_accessed=8 * MIB, transcendentals=0
        ),
        name="flash",
    )(pos, bases, *args)


def unpack_lse(ref):
    tail = ref[ROWS : ROWS + EXT, :].astype(jnp.float32)
    return tail[0:8, :] + tail[8:16, :] + tail[16:24, :]


def merge_kernel(final, a_ref, b_ref, o_ref, *scratch):
    lse_a, lse_b = unpack_lse(a_ref), unpack_lse(b_ref)
    top = jnp.maximum(lse_a, lse_b)
    weight_a, weight_b = jnp.exp2(lse_a - top), jnp.exp2(lse_b - top)
    total = weight_a + weight_b
    part_a, part_b = weight_a / total, weight_b / total
    eye = lax.broadcasted_iota(jnp.int32, (HEAD, HEAD), 0) == lax.broadcasted_iota(
        jnp.int32, (HEAD, HEAD), 1
    )

    def spread(line):
        return jnp.sum(jnp.where(eye, line, 0.0), axis=1, keepdims=True)

    for j in range(ROWS // HEAD):
        r = j * HEAD
        x = spread(part_a[j : j + 1, :]) * a_ref[r : r + HEAD, :].astype(jnp.float32)
        x += spread(part_b[j : j + 1, :]) * b_ref[r : r + HEAD, :].astype(jnp.float32)
        x = x.astype(jnp.bfloat16)
        if final:
            for g in range(2):
                cols = (2 * j + g) * HEAD
                o_ref[:, cols : cols + HEAD] = x[g * TOK : (g + 1) * TOK, :]
        else:
            o_ref[r : r + HEAD, :] = x
    if not final:
        lse = top + jnp.log2(total)
        hi = lse.astype(jnp.bfloat16).astype(jnp.float32)
        mid = (lse - hi).astype(jnp.bfloat16).astype(jnp.float32)
        low = lse - hi - mid
        tail = jnp.concatenate([hi, mid, low, jnp.zeros_like(lse)], axis=0)
        o_ref[ROWS : ROWS + EXT, :] = tail.astype(jnp.bfloat16)


def merge(a, b, final):
    shape = (TOK, GROUP * HEAD) if final else (ROWS + EXT, HEAD)
    return pl.pallas_call(
        functools.partial(merge_kernel, final),
        out_shape=jax.ShapeDtypeStruct(shape, jnp.bfloat16),
        in_specs=[pl.BlockSpec(memory_space=VMEM)] * 2,
        out_specs=pl.BlockSpec(memory_space=VMEM),
        name="merge",
    )(a, b)


def project_kernel(me_ref, *refs):
    x_refs, w_refs, o_ref, held = refs[:9], refs[9:13], refs[13], refs[14]
    z, r = me_ref[0], me_ref[1]
    at = 0
    for x in x_refs:
        held[at : at + x.shape[0], :] = x[...]
        at += x.shape[0]
    places = [0, -1, 1, -2, 2, -3, 3, 4]
    for i in range(NR):
        piece = jnp.bitwise_xor(r, i)
        for c in range(0, 512, 256):
            y = jnp.dot(
                held[...], w_refs[i][:, c : c + 256], preferred_element_type=jnp.float32
            ).astype(jnp.bfloat16)
            for j, place in enumerate(places):
                owner = lax.rem(z + place + NZ, NZ)
                o_ref[piece * NZ + owner, :, c : c + 256] = y[j * TOK : (j + 1) * TOK, :]


def project(me, xs, ws):
    cols = ws[0].shape[1]
    return pl.pallas_call(
        project_kernel,
        out_shape=jax.ShapeDtypeStruct((NR * NZ, TOK, cols), jnp.bfloat16),
        in_specs=[pl.BlockSpec(memory_space=SMEM)]
        + [pl.BlockSpec(memory_space=VMEM)] * (len(xs) + len(ws)),
        out_specs=pl.BlockSpec(memory_space=VMEM),
        scratch_shapes=[VMEM((NZ * TOK, GROUP * HEAD), jnp.bfloat16)],
        compiler_params=pltpu.CompilerParams(vmem_limit_bytes=40 * MIB),
        name="project",
    )(me, *xs, *ws)


def ring(x):
    half = x.shape[0] // 2
    up = down = x
    got = []
    for _ in range(3):
        up, down = move(up, z_shift(1)), move(down, z_shift(-1))
        got.append((up, down))
    got.append((move(up[:half], z_shift(1)), move(down[half:], z_shift(-1))))
    return got


def shards(queries, keys, values, out_weight, cache_len, block_order):
    blk = lax.axis_index("blk")
    z, r = blk // NR, blk % NR
    kv = jnp.concatenate([keys, values], axis=1)
    kv_got = ring(kv)
    q0 = prep(block_order, queries)
    q1 = move(q0, swap(1))
    q2 = move(q0, swap(2))
    q3 = move(q2, swap(1))
    w0 = out_weight
    w1 = move(w0, swap(1))
    w2 = move(w0, swap(2))
    w3 = move(w2, swap(1))
    qs = jnp.stack([q0, q1, q2, q3])
    pos = cache_len[0] + TOK * qs[:, ROWS, 0].astype(jnp.int32)

    def base_of(distance):
        return (((z + distance + NZ) % NZ) * NR + r) * C_ROWS

    def bases(*items):
        return jnp.stack(items).astype(jnp.int32)

    state = flash(pos, bases(base_of(0)), qs, [kv], None, False)
    for step in range(2):
        where = bases(base_of(-1 - step), base_of(1 + step))
        state = flash(pos, where, qs, list(kv_got[step]), state, False)
    where = bases(base_of(-3), base_of(3), base_of(4), base_of(4) + C_ROWS // 2)
    packed = flash(pos, where, qs, list(kv_got[2] + kv_got[3]), state, True)
    from_core = move(packed[1::2], swap(1))
    near = merge(packed[0], from_core[0], False)
    far = merge(packed[2], from_core[1], False)
    attn = merge(near, move(far, swap(2)), True)

    got = ring(attn)
    xs = [attn] + [x for pair in got for x in pair]
    terms = project(jnp.stack([z, r]).astype(jnp.int32), xs, [w0, w1, w2, w3])
    groups = [
        [(zz * NR + rr) * 8 + h for rr in range(NR) for h in range(8)] for zz in range(NZ)
    ]
    parts = lax.all_to_all(
        terms, ("blk", "head"), 0, 0, tiled=True, axis_index_groups=groups
    )
    parts = parts.reshape(NR, 8, TOK, parts.shape[-1])
    total = jnp.sum(parts.astype(jnp.float32), axis=1)
    return total.reshape(NR * TOK, -1).astype(jnp.bfloat16)


def solution(mesh):
    return jax.shard_map(
        shards,
        mesh=mesh,
        in_specs=(
            P("blk", "head"),
            P("blk", "head"),
            P("blk", "head"),
            P("head", "blk"),
            P(),
            P("blk"),
        ),
        out_specs=P("head", "blk"),
        check_vma=False,
    )
```

```python
import functools
import math

import jax
import jax.numpy as jnp
from jax import lax
from jax.experimental import pallas as pl
from jax.experimental.pallas import tpu as pltpu
from jax.sharding import PartitionSpec as P

HEAD = 128
GROUP = 16
TOK = 64
ROWS = GROUP * TOK
C_ROWS = 512
SCALE = math.log2(math.e) / math.sqrt(HEAD)
LOW = -1e30
RB = 256
STEP = 1024
NZ, NR = 8, 4
EXT = 32
MIB = 2**20
VMEM = pltpu.VMEM
SMEM = pltpu.SMEM


def z_shift(step):
    return [(z * NR + r, ((z + step) % NZ) * NR + r) for z in range(NZ) for r in range(NR)]


def swap(bit):
    return [(b, b ^ bit) for b in range(NZ * NR)]


def move(x, pairs):
    return lax.ppermute(x, "blk", pairs)


def later(x, event):
    return lax.optimization_barrier((x, event))[0]


def prep_kernel(order_ref, q_ref, k_ref, v_ref, o_ref, kv_ref, sem):
    copies = [
        pltpu.make_async_copy(k_ref, kv_ref.at[:C_ROWS], sem.at[GROUP]),
        pltpu.make_async_copy(v_ref, kv_ref.at[C_ROWS:], sem.at[GROUP + 1]),
    ]
    for g in range(GROUP):
        rows, cols = pl.ds(g * TOK, TOK), pl.ds(g * HEAD, HEAD)
        copies.append(pltpu.make_async_copy(q_ref.at[:, cols], o_ref.at[rows], sem.at[g]))
    for copy in copies:
        copy.start()
    place = jnp.full((16, HEAD), order_ref[0], jnp.int32).astype(jnp.float32)
    o_ref[ROWS : ROWS + 16, :] = place.astype(jnp.bfloat16)
    for copy in copies:
        copy.wait()


def prep(order, queries, keys, values):
    return pl.pallas_call(
        prep_kernel,
        out_shape=[
            jax.ShapeDtypeStruct((ROWS + 16, HEAD), jnp.bfloat16),
            jax.ShapeDtypeStruct((2 * C_ROWS, HEAD), jnp.bfloat16),
        ],
        in_specs=[pl.BlockSpec(memory_space=SMEM)] + [pl.BlockSpec(memory_space=pl.ANY)] * 3,
        out_specs=[pl.BlockSpec(memory_space=VMEM)] * 2,
        scratch_shapes=[pltpu.SemaphoreType.DMA((GROUP + 2,))],
        compiler_params=pltpu.CompilerParams(vmem_limit_bytes=8 * MIB),
        name="prep",
    )(order, queries, keys, values)


def compact(x):
    eye = lax.broadcasted_iota(jnp.int32, (HEAD, HEAD), 0) == lax.broadcasted_iota(
        jnp.int32, (HEAD, HEAD), 1
    )
    return jnp.sum(jnp.where(eye, x, 0.0), axis=0, keepdims=True)


def spread(line):
    return jnp.broadcast_to(line, (HEAD, HEAD)).T


def write_lse(o_ref, lse):
    hi = lse.astype(jnp.bfloat16).astype(jnp.float32)
    mid = (lse - hi).astype(jnp.bfloat16).astype(jnp.float32)
    low = lse - hi - mid
    tail = jnp.concatenate([hi, mid, low, jnp.zeros_like(lse)], axis=0)
    o_ref[ROWS : ROWS + EXT, :] = tail.astype(jnp.bfloat16)


def read_lse(ref):
    tail = ref[ROWS : ROWS + EXT, :].astype(jnp.float32)
    return tail[0:8, :] + tail[8:16, :] + tail[16:24, :]


def pack(o_ref, acc, top, other):
    lines = []
    other_lse = None if other is None else read_lse(other)
    for j in range(ROWS // HEAD):
        rows = slice(j * HEAD, (j + 1) * HEAD)
        total = acc[rows, HEAD:]
        x = acc[rows, :HEAD] / total
        lse = top[rows, :] + jnp.log2(total)
        if other is not None:
            lse_b = spread(other_lse[j : j + 1, :])
            highest = jnp.maximum(lse, lse_b)
            weight_a, weight_b = jnp.exp2(lse - highest), jnp.exp2(lse_b - highest)
            both = weight_a + weight_b
            x = (weight_a * x + weight_b * other[rows, :].astype(jnp.float32)) / both
            lse = highest + jnp.log2(both)
        o_ref[rows, :] = x.astype(jnp.bfloat16)
        lines.append(compact(lse))
    write_lse(o_ref, jnp.concatenate(lines, axis=0))


def absorb(q, keys, values, into, origin, rows_at, count, first_key, size, pos):
    acc, top = into
    halves = STEP // RB

    def scores(row):
        k = keys[pl.ds(first_key, size), :]
        s = lax.dot_general(
            q[pl.ds(row, RB), :], k, (((1,), (1,)), ((), ())), preferred_element_type=jnp.float32
        )
        s = s * SCALE
        if pos is not None:
            line = lax.broadcasted_iota(jnp.int32, (RB, size), 0) % TOK
            col = lax.broadcasted_iota(jnp.int32, (RB, size), 1)
            s = jnp.where(pos[1] + col <= pos[0] + line, s, LOW)
        return s

    def weigh(row, s):
        new = jnp.max(s, axis=1, keepdims=True)
        shrink = None
        if origin is None:
            new = jnp.broadcast_to(new, (RB, HEAD))
        else:
            old = origin[1][pl.ds(row, RB), :]
            new = jnp.maximum(old, new)
            shrink = jnp.exp2(old - new)
        top[pl.ds(row, RB), :] = new
        p = jnp.exp2(s - jnp.tile(new, (1, size // HEAD))).astype(jnp.bfloat16)
        return p, shrink

    def add(row, p, shrink):
        v1 = values[pl.ds(first_key, size), :]
        more = jnp.dot(p, v1, preferred_element_type=jnp.float32)
        if origin is not None:
            more += origin[0][pl.ds(row, RB), :] * jnp.tile(shrink, (1, 2))
        acc[pl.ds(row, RB), :] = more

    def step(t, carry):
        row = lambda i: pl.multiple_of(rows_at + t * STEP + i * RB, RB)
        s, held = scores(row(0)), None
        for i in range(halves):
            later = scores(row(i + 1)) if i + 1 < halves else None
            p, shrink = weigh(row(i), s)
            if held is not None:
                add(*held)
            held, s = (row(i), p, shrink), later
        add(*held)
        return carry

    lax.fori_loop(0, count, step, 0)


def flash_kernel(blocks, slot, with_other, n_after, info_ref, *refs):
    n = sum(len(block) for block in blocks)
    last = slot is not None
    n_q = 1 if last else 2
    kv_refs, q_refs, refs = refs[:n], refs[n : n + n_q], refs[n + n_q :]
    fresh = not last and len(refs) == 5 + n_after
    other = origin = None
    if not fresh:
        origin, refs = refs[:2], refs[2:]
    if with_other:
        other, refs = refs[0], refs[1:]
    refs = refs[n_after:]
    if last:
        out_ref, acc, top, q, keys, values = refs
        origin = (origin[0].at[pl.ds(slot * ROWS, ROWS)], origin[1].at[pl.ds(slot * ROWS, ROWS)])
    else:
        acc, top, q, keys, values = refs
    into = (acc, top)
    for j, ref in enumerate(kv_refs):
        rows = slice(j * C_ROWS, (j + 1) * C_ROWS)
        keys[rows, :] = ref[:C_ROWS, :]
        values[rows, :HEAD] = ref[C_ROWS:, :]
    values[:, HEAD:] = jnp.ones((n * C_ROWS, HEAD), jnp.bfloat16)
    z, r, cached = info_ref[0], info_ref[1], info_ref[2]
    way = 1 - 2 * jnp.bitwise_and(r, 1)
    pos = []
    for i, ref in enumerate(q_refs):
        q[i * ROWS : (i + 1) * ROWS, :] = ref[:ROWS, :]
        place = jnp.max(ref[ROWS : ROWS + 16, :].astype(jnp.float32)).astype(jnp.int32)
        pos.append(cached + TOK * place)

    def base_of(piece):
        return (
            lax.rem(z + NZ - piece[0] * way, NZ) * NR + jnp.bitwise_xor(r, piece[1])
        ) * C_ROWS

    at = 0
    for b, block in enumerate(blocks):
        start = into if b else origin
        first_key = at * C_ROWS
        bases = [base_of(piece) for piece in block]
        end = functools.reduce(jnp.maximum, bases) + C_ROWS - 1
        seen = end <= functools.reduce(jnp.minimum, pos)

        @pl.when(seen)
        def _():
            whole = len(block) * C_ROWS
            steps = n_q * ROWS // STEP
            absorb(q, keys, values, into, start, 0, steps, first_key, whole, None)

        @pl.when(jnp.logical_not(seen))
        def _():
            if start is None:
                acc[...] = jnp.zeros(acc.shape, jnp.float32)
                top[...] = jnp.full(top.shape, LOW, jnp.float32)
            elif start is not into:
                acc[...] = start[0][...]
                top[...] = start[1][...]

            def one(j, carry):
                i, piece = (0, j) if n_q == 1 else (j % 2, j // 2)
                first = pos[0] if n_q == 1 else jnp.where(i == 0, pos[0], pos[1])
                base = bases[0] if len(block) == 1 else jnp.where(piece == 0, *bases)
                key = pl.multiple_of(first_key + piece * C_ROWS, C_ROWS)

                @pl.when(base <= first + TOK - 1)
                def _():
                    steps = ROWS // STEP
                    where = (first, base)
                    absorb(q, keys, values, into, into, i * ROWS, steps, key, C_ROWS, where)

                return carry

            lax.fori_loop(0, n_q * len(block), one, 0)

        at += len(block)

    if last:
        pack(out_ref, acc, top, other)


def flash(info, blocks, kvs, queries, state, slot=None, other=None, after=()):
    n = len(kvs)
    whole = pl.BlockSpec(memory_space=VMEM)
    last = slot is not None
    if last:
        queries = queries[slot : slot + 1]
    args = [info, *kvs, *queries]
    aliases = {}
    if state is not None:
        if not last:
            aliases = {len(args): 0, len(args) + 1: 1}
        args += list(state)
    if other is not None:
        args.append(other)
    in_specs = [pl.BlockSpec(memory_space=SMEM)] + [whole] * (len(args) - 1)
    args += list(after)
    in_specs += [pl.BlockSpec(memory_space=pl.ANY)] * len(after)
    n_q = 1 if last else 2
    scratch = [
        VMEM((n_q * ROWS, HEAD), jnp.bfloat16),
        VMEM((n * C_ROWS, HEAD), jnp.bfloat16),
        VMEM((n * C_ROWS, 2 * HEAD), jnp.bfloat16),
    ]
    if last:
        out_shape = jax.ShapeDtypeStruct((ROWS + EXT, HEAD), jnp.bfloat16)
        out_specs = whole
        scratch = [
            VMEM((ROWS, 2 * HEAD), jnp.float32),
            VMEM((ROWS, HEAD), jnp.float32),
        ] + scratch
    else:
        out_shape = [
            jax.ShapeDtypeStruct((2 * ROWS, 2 * HEAD), jnp.float32),
            jax.ShapeDtypeStruct((2 * ROWS, HEAD), jnp.float32),
        ]
        out_specs = [whole] * 2
    return pl.pallas_call(
        functools.partial(flash_kernel, blocks, slot, other is not None, len(after)),
        out_shape=out_shape,
        in_specs=in_specs,
        out_specs=out_specs,
        scratch_shapes=scratch,
        input_output_aliases=aliases,
        compiler_params=pltpu.CompilerParams(vmem_limit_bytes=24 * MIB),
        cost_estimate=pl.CostEstimate(
            flops=n_q * ROWS * n * C_ROWS * HEAD * 16, bytes_accessed=4 * MIB, transcendentals=0
        ),
        name="flash",
    )(*args)


def merge_kernel(a_ref, b_ref, o_ref):
    lse_a, lse_b = read_lse(a_ref), read_lse(b_ref)
    top = jnp.maximum(lse_a, lse_b)
    weight_a, weight_b = jnp.exp2(lse_a - top), jnp.exp2(lse_b - top)
    part_a = weight_a / (weight_a + weight_b)
    part_b = weight_b / (weight_a + weight_b)
    for j in range(ROWS // HEAD):
        rows = slice(j * HEAD, (j + 1) * HEAD)
        x = spread(part_a[j : j + 1, :]) * a_ref[rows, :].astype(jnp.float32)
        x += spread(part_b[j : j + 1, :]) * b_ref[rows, :].astype(jnp.float32)
        x = x.astype(jnp.bfloat16)
        for g in range(2):
            cols = (2 * j + g) * HEAD
            o_ref[:, cols : cols + HEAD] = x[g * TOK : (g + 1) * TOK, :]


def merge(a, b):
    return pl.pallas_call(
        merge_kernel,
        out_shape=jax.ShapeDtypeStruct((TOK, GROUP * HEAD), jnp.bfloat16),
        in_specs=[pl.BlockSpec(memory_space=VMEM)] * 2,
        out_specs=pl.BlockSpec(memory_space=VMEM),
        compiler_params=pltpu.CompilerParams(vmem_limit_bytes=8 * MIB),
        name="merge",
    )(a, b)


def project_kernel(places, more, info_ref, *refs):
    n = len(places)
    x_refs, w_refs, refs = refs[: n], refs[n : n + NR], refs[n + NR :]
    o_ref, held = refs[-2], refs[-1]
    z, r = info_ref[0], info_ref[1]
    if more:
        o_ref[...] = refs[0][...]
    at = 0
    for x in x_refs:
        held[at : at + x.shape[0], :] = x[...]
        at += x.shape[0]
    for i in range(NR):
        piece = jnp.bitwise_xor(r, i)
        for c in range(0, 512, 256):
            cols = slice(c, c + 256)
            y = jnp.dot(held[...], w_refs[i][:, cols], preferred_element_type=jnp.float32)
            y = y.astype(jnp.bfloat16)
            at = 0
            for place, start, x in [(p, s, x) for (p, s), x in zip(places, x_refs)]:
                size = x.shape[0]
                owner = lax.rem(z + place + NZ, NZ)
                o_ref[piece * NZ + owner, start : start + size, cols] = y[at : at + size, :]
                at += size


def project(info, xs, places, ws, terms):
    cols = ws[0].shape[1]
    rows = sum(x.shape[0] for x in xs)
    args = [info, *xs, *ws]
    more = terms is not None
    if more:
        args.append(terms)
    return pl.pallas_call(
        functools.partial(project_kernel, places, more),
        out_shape=jax.ShapeDtypeStruct((NR * NZ, TOK, cols), jnp.bfloat16),
        in_specs=[pl.BlockSpec(memory_space=SMEM)]
        + [pl.BlockSpec(memory_space=VMEM)] * (len(args) - 1),
        out_specs=pl.BlockSpec(memory_space=VMEM),
        scratch_shapes=[VMEM((rows, GROUP * HEAD), jnp.bfloat16)],
        input_output_aliases={len(args) - 1: 0} if more else {},
        compiler_params=pltpu.CompilerParams(vmem_limit_bytes=24 * MIB),
        cost_estimate=pl.CostEstimate(
            flops=2 * rows * 2048 * 2048 * 2, bytes_accessed=12 * MIB, transcendentals=0
        ),
        name="project",
    )(*args)


def ring(x):
    half = x.shape[0] // 2
    up = down = x
    got = []
    for _ in range(3):
        up, down = move(up, z_shift(1)), move(down, z_shift(-1))
        got.append((up, down))
    got.append((move(up[:half], z_shift(1)), move(down[half:], z_shift(-1))))
    return got


def shards(queries, keys, values, out_weight, cache_len, block_order):
    blk = lax.axis_index("blk")
    info = jnp.stack([blk // NR, blk % NR, cache_len[0]]).astype(jnp.int32)
    q0, kv0 = prep(block_order, queries, keys, values)
    around = [
        (at * NR + r, ((at + 1 - 2 * (r % 2)) % NZ) * NR + r)
        for at in range(NZ)
        for r in range(NR)
    ]
    x1 = move(kv0, around)
    kv1 = move(kv0, swap(1))
    q1 = move(q0, swap(1))
    y1 = move(kv1, around)
    q2 = move(q0, swap(2))
    q3 = move(q2, swap(1))
    w0 = out_weight
    w1 = move(w0, swap(1))
    w2 = move(w0, swap(2))

    pair = lambda s: ((s, 0), (s, 1))
    own = ((0, 0),)
    near_q, far_q = [q0, q1], [q2, q3]
    near = flash(info, [own], [kv0], near_q, None)
    x2 = move(later(x1, near[1]), around)
    y2 = move(y1, around)
    near = flash(info, [pair(1)], [x1, y1], near_q, near)
    x3, y3 = move(later(x2, near[1]), around), move(later(y2, near[1]), around)
    far = flash(info, [own, pair(1)], [kv0, x1, y1], far_q, None, after=near[1:])
    near = flash(info, [pair(2)], [x2, y2], near_q, near, after=far[1:])
    x4 = move(x3, around)
    far = flash(info, [pair(2)], [x2, y2], far_q, far, after=near[1:])
    near = flash(info, [pair(3)], [x3, y3], near_q, near, after=far[1:])
    far = flash(info, [pair(3)], [x3, y3], far_q, far, after=near[1:])
    final = functools.partial(flash, info, [((4, 0),)], [x4])
    p3 = final(far_q, far, 1)
    p1 = final(near_q, near, 1, after=(p3,))
    p2 = final(far_q, far, 0, other=move(p3, swap(1)), after=(p1,))
    p1_there = move(p1, swap(1))
    far_there = move(later(p2, p1_there), swap(2))
    p0 = final(near_q, near, 0, other=p1_there, after=(p2,))
    attn = merge(p0, far_there)

    w3 = move(later(w2, p0), swap(1))
    ws = [w0, w1, w2, w3]
    got = ring(attn)
    xs = [attn, *got[0], *got[1]]
    places = [(0, 0), (-1, 0), (1, 0), (-2, 0), (2, 0)]
    terms = project(info, xs, places, ws, None)
    xs = [*got[2], *got[3]]
    places = [(-3, 0), (3, 0), (4, 0), (4, TOK // 2)]
    terms = project(info, xs, places, ws, terms)
    groups = [
        [(zz * NR + rr) * 8 + h for rr in range(NR) for h in range(8)] for zz in range(NZ)
    ]
    parts = lax.all_to_all(
        terms, ("blk", "head"), 0, 0, tiled=True, axis_index_groups=groups
    )
    parts = parts.reshape(NR, 8, TOK, parts.shape[-1])
    total = jnp.sum(parts.astype(jnp.float32), axis=1)
    return total.reshape(NR * TOK, -1).astype(jnp.bfloat16)


def solution(mesh):
    return jax.shard_map(
        shards,
        mesh=mesh,
        in_specs=(
            P("blk", "head"),
            P("blk", "head"),
            P("blk", "head"),
            P("head", "blk"),
            P(),
            P("blk"),
        ),
        out_specs=P("head", "blk"),
        check_vma=False,
    )
```

```python
import functools
import math

import jax
import jax.numpy as jnp
from jax import lax
from jax.experimental import pallas as pl
from jax.experimental.pallas import tpu as pltpu
from jax.sharding import PartitionSpec as P

HEAD = 128
GROUP = 16
TOK = 64
ROWS = GROUP * TOK
C_ROWS = 512
SCALE = math.log2(math.e) / math.sqrt(HEAD)
LOW = -1e30
RB = 256
STEP = 1024
NZ, NR = 8, 4
EXT = 32
MIB = 2**20
VMEM = pltpu.VMEM
SMEM = pltpu.SMEM


def z_shift(step):
    return [(z * NR + r, ((z + step) % NZ) * NR + r) for z in range(NZ) for r in range(NR)]


def swap(bit):
    return [(b, b ^ bit) for b in range(NZ * NR)]


def move(x, pairs):
    return lax.ppermute(x, "blk", pairs)


def later(x, event):
    return lax.optimization_barrier((x, event))[0]


def prep_kernel(order_ref, q_ref, k_ref, v_ref, o_ref, kv_ref, sem):
    copies = [
        pltpu.make_async_copy(k_ref, kv_ref.at[:C_ROWS], sem.at[GROUP]),
        pltpu.make_async_copy(v_ref, kv_ref.at[C_ROWS:], sem.at[GROUP + 1]),
    ]
    for g in range(GROUP):
        rows, cols = pl.ds(g * TOK, TOK), pl.ds(g * HEAD, HEAD)
        copies.append(pltpu.make_async_copy(q_ref.at[:, cols], o_ref.at[rows], sem.at[g]))
    for copy in copies:
        copy.start()
    place = jnp.full((16, HEAD), order_ref[0], jnp.int32).astype(jnp.float32)
    o_ref[ROWS : ROWS + 16, :] = place.astype(jnp.bfloat16)
    for copy in copies:
        copy.wait()


def prep(order, queries, keys, values):
    return pl.pallas_call(
        prep_kernel,
        out_shape=[
            jax.ShapeDtypeStruct((ROWS + 16, HEAD), jnp.bfloat16),
            jax.ShapeDtypeStruct((2 * C_ROWS, HEAD), jnp.bfloat16),
        ],
        in_specs=[pl.BlockSpec(memory_space=SMEM)] + [pl.BlockSpec(memory_space=pl.ANY)] * 3,
        out_specs=[pl.BlockSpec(memory_space=VMEM)] * 2,
        scratch_shapes=[pltpu.SemaphoreType.DMA((GROUP + 2,))],
        compiler_params=pltpu.CompilerParams(vmem_limit_bytes=56 * MIB),
        name="prep",
    )(order, queries, keys, values)


def compact(x):
    eye = lax.broadcasted_iota(jnp.int32, (HEAD, HEAD), 0) == lax.broadcasted_iota(
        jnp.int32, (HEAD, HEAD), 1
    )
    return jnp.sum(jnp.where(eye, x, 0.0), axis=0, keepdims=True)


def spread(line):
    return jnp.broadcast_to(line, (HEAD, HEAD)).T


def write_lse(o_ref, lse):
    hi = lse.astype(jnp.bfloat16).astype(jnp.float32)
    mid = (lse - hi).astype(jnp.bfloat16).astype(jnp.float32)
    low = lse - hi - mid
    tail = jnp.concatenate([hi, mid, low, jnp.zeros_like(lse)], axis=0)
    o_ref[ROWS : ROWS + EXT, :] = tail.astype(jnp.bfloat16)


def read_lse(ref):
    tail = ref[ROWS : ROWS + EXT, :].astype(jnp.float32)
    return tail[0:8, :] + tail[8:16, :] + tail[16:24, :]


def pack(o_ref, acc, top, first):
    lines = []
    for j in range(ROWS // HEAD):
        held = slice(first + j * HEAD, first + (j + 1) * HEAD)
        total = acc[held, HEAD:]
        x = acc[held, :HEAD] / total
        o_ref[j * HEAD : (j + 1) * HEAD, :] = x.astype(jnp.bfloat16)
        lines.append(compact(top[held, :] + jnp.log2(total)))
    write_lse(o_ref, jnp.concatenate(lines, axis=0))


def absorb(q, keys, values, into, origin, rows_at, count, first_key, size, pos):
    acc, top = into
    halves = STEP // RB

    def scores(row):
        k = keys[pl.ds(first_key, size), :]
        s = lax.dot_general(
            q[pl.ds(row, RB), :], k, (((1,), (1,)), ((), ())), preferred_element_type=jnp.float32
        )
        s = s * SCALE
        if pos is not None:
            line = lax.broadcasted_iota(jnp.int32, (RB, size), 0) % TOK
            col = lax.broadcasted_iota(jnp.int32, (RB, size), 1)
            s = jnp.where(pos[1] + col <= pos[0] + line, s, LOW)
        return s

    def weigh(row, s):
        new = jnp.max(s, axis=1, keepdims=True)
        shrink = None
        if origin is None:
            new = jnp.broadcast_to(new, (RB, HEAD))
        else:
            old = origin[1][pl.ds(row, RB), :]
            new = jnp.maximum(old, new)
            shrink = jnp.exp2(old - new)
        top[pl.ds(row, RB), :] = new
        p = jnp.exp2(s - jnp.tile(new, (1, size // HEAD))).astype(jnp.bfloat16)
        return p, shrink

    def add(row, p, shrink):
        v1 = values[pl.ds(first_key, size), :]
        more = jnp.dot(p, v1, preferred_element_type=jnp.float32)
        if origin is not None:
            more += origin[0][pl.ds(row, RB), :] * jnp.tile(shrink, (1, 2))
        acc[pl.ds(row, RB), :] = more

    def step(t, carry):
        row = lambda i: pl.multiple_of(rows_at + t * STEP + i * RB, RB)
        s, held = scores(row(0)), None
        for i in range(halves):
            later = scores(row(i + 1)) if i + 1 < halves else None
            p, shrink = weigh(row(i), s)
            if held is not None:
                add(*held)
            held, s = (row(i), p, shrink), later
        add(*held)
        return carry

    lax.fori_loop(0, count, step, 0)


def flash_kernel(blocks, last, n_after, info_ref, *refs):
    n = sum(len(block) for block in blocks)
    n_q = 2
    kv_refs, q_refs, refs = refs[:n], refs[n : n + n_q], refs[n + n_q :]
    fresh = not last and len(refs) == 5 + n_after
    origin = None
    if not fresh:
        origin, refs = refs[:2], refs[2:]
    refs = refs[n_after:]
    if last:
        out_refs, refs = refs[:2], refs[2:]
    acc, top, q, keys, values = refs
    into = (acc, top)
    for j, ref in enumerate(kv_refs):
        rows = slice(j * C_ROWS, (j + 1) * C_ROWS)
        keys[rows, :] = ref[:C_ROWS, :]
        values[rows, :HEAD] = ref[C_ROWS:, :]
    values[:, HEAD:] = jnp.ones((n * C_ROWS, HEAD), jnp.bfloat16)
    z, r, cached = info_ref[0], info_ref[1], info_ref[2]
    way = 1 - 2 * jnp.bitwise_and(r, 1)
    pos = []
    for i, ref in enumerate(q_refs):
        q[i * ROWS : (i + 1) * ROWS, :] = ref[:ROWS, :]
        place = jnp.max(ref[ROWS : ROWS + 16, :].astype(jnp.float32)).astype(jnp.int32)
        pos.append(cached + TOK * place)

    def base_of(piece):
        return (
            lax.rem(z + NZ - piece[0] * way, NZ) * NR + jnp.bitwise_xor(r, piece[1])
        ) * C_ROWS

    at = 0
    for b, block in enumerate(blocks):
        start = into if b else origin
        first_key = at * C_ROWS
        bases = [base_of(piece) for piece in block]
        end = functools.reduce(jnp.maximum, bases) + C_ROWS - 1
        seen = end <= functools.reduce(jnp.minimum, pos)

        @pl.when(seen)
        def _():
            whole = len(block) * C_ROWS
            steps = n_q * ROWS // STEP
            absorb(q, keys, values, into, start, 0, steps, first_key, whole, None)

        @pl.when(jnp.logical_not(seen))
        def _():
            if start is None:
                acc[...] = jnp.zeros(acc.shape, jnp.float32)
                top[...] = jnp.full(top.shape, LOW, jnp.float32)
            elif start is not into:
                acc[...] = start[0][...]
                top[...] = start[1][...]

            def one(j, carry):
                i, piece = j % 2, j // 2
                first = jnp.where(i == 0, pos[0], pos[1])
                base = bases[0] if len(block) == 1 else jnp.where(piece == 0, *bases)
                key = pl.multiple_of(first_key + piece * C_ROWS, C_ROWS)

                @pl.when(base <= first + TOK - 1)
                def _():
                    steps = ROWS // STEP
                    where = (first, base)
                    absorb(q, keys, values, into, into, i * ROWS, steps, key, C_ROWS, where)

                return carry

            lax.fori_loop(0, n_q * len(block), one, 0)

        at += len(block)

    if last:
        for i in range(n_q):
            pack(out_refs[i], acc, top, i * ROWS)


def flash(info, blocks, kvs, queries, state, last=False, after=()):
    n = len(kvs)
    whole = pl.BlockSpec(memory_space=VMEM)
    args = [info, *kvs, *queries]
    aliases = {}
    if state is not None:
        if not last:
            aliases = {len(args): 0, len(args) + 1: 1}
        args += list(state)
    in_specs = [pl.BlockSpec(memory_space=SMEM)] + [whole] * (len(args) - 1)
    args += list(after)
    in_specs += [pl.BlockSpec(memory_space=pl.ANY)] * len(after)
    scratch = [
        VMEM((2 * ROWS, HEAD), jnp.bfloat16),
        VMEM((n * C_ROWS, HEAD), jnp.bfloat16),
        VMEM((n * C_ROWS, 2 * HEAD), jnp.bfloat16),
    ]
    if last:
        out_shape = [jax.ShapeDtypeStruct((ROWS + EXT, HEAD), jnp.bfloat16)] * 2
        scratch = [
            VMEM((2 * ROWS, 2 * HEAD), jnp.float32),
            VMEM((2 * ROWS, HEAD), jnp.float32),
        ] + scratch
    else:
        out_shape = [
            jax.ShapeDtypeStruct((2 * ROWS, 2 * HEAD), jnp.float32),
            jax.ShapeDtypeStruct((2 * ROWS, HEAD), jnp.float32),
        ]
    return pl.pallas_call(
        functools.partial(flash_kernel, blocks, last, len(after)),
        out_shape=out_shape,
        in_specs=in_specs,
        out_specs=[whole] * 2,
        scratch_shapes=scratch,
        input_output_aliases=aliases,
        compiler_params=pltpu.CompilerParams(vmem_limit_bytes=24 * MIB),
        cost_estimate=pl.CostEstimate(
            flops=2 * ROWS * n * C_ROWS * HEAD * 16, bytes_accessed=4 * MIB, transcendentals=0
        ),
        name="flash",
    )(*args)


def merge_kernel(final, *refs):
    parts, o_ref = refs[:-1], refs[-1]
    lses = [read_lse(ref) for ref in parts]
    top = functools.reduce(jnp.maximum, lses)
    weights = [jnp.exp2(lse - top) for lse in lses]
    total = functools.reduce(jnp.add, weights)
    shares = [weight / total for weight in weights]
    for j in range(ROWS // HEAD):
        rows = slice(j * HEAD, (j + 1) * HEAD)
        x = jnp.zeros((HEAD, HEAD), jnp.float32)
        for share, ref in zip(shares, parts):
            x += spread(share[j : j + 1, :]) * ref[rows, :].astype(jnp.float32)
        x = x.astype(jnp.bfloat16)
        if final:
            for g in range(2):
                cols = (2 * j + g) * HEAD
                o_ref[:, cols : cols + HEAD] = x[g * TOK : (g + 1) * TOK, :]
        else:
            o_ref[rows, :] = x
    if not final:
        write_lse(o_ref, top + jnp.log2(total))


def merge(parts, final):
    shape = (TOK, GROUP * HEAD) if final else (ROWS + EXT, HEAD)
    return pl.pallas_call(
        functools.partial(merge_kernel, final),
        out_shape=jax.ShapeDtypeStruct(shape, jnp.bfloat16),
        in_specs=[pl.BlockSpec(memory_space=VMEM)] * len(parts),
        out_specs=pl.BlockSpec(memory_space=VMEM),
        compiler_params=pltpu.CompilerParams(vmem_limit_bytes=8 * MIB),
        name="merge",
    )(*parts)


W_CUT = 1024


def project_kernel(places, more, info_ref, *refs):
    n = len(places)
    x_refs, w_refs, refs = refs[: n], refs[n : n + 6], refs[n + 6 :]
    o_ref, held = refs[-2], refs[-1]
    z, r = info_ref[0], info_ref[1]
    if more:
        o_ref[...] = refs[0][...]
    at = 0
    for x in x_refs:
        held[at : at + x.shape[0], :] = x[...]
        at += x.shape[0]
    for i in range(NR):
        piece = jnp.bitwise_xor(r, i)
        for c in range(0, 512, 256):
            cols = slice(c, c + 256)
            if i < 2:
                y = jnp.dot(held[...], w_refs[i][:, cols], preferred_element_type=jnp.float32)
            else:
                upper, lower = w_refs[2 * i - 2], w_refs[2 * i - 1]
                y = jnp.dot(
                    held[:, :W_CUT], upper[:, cols], preferred_element_type=jnp.float32
                ) + jnp.dot(
                    held[:, W_CUT:], lower[:, cols], preferred_element_type=jnp.float32
                )
            y = y.astype(jnp.bfloat16)
            at = 0
            for place, start, x in [(p, s, x) for (p, s), x in zip(places, x_refs)]:
                size = x.shape[0]
                owner = lax.rem(z + NZ + place, NZ)
                o_ref[piece * NZ + owner, start : start + size, cols] = y[at : at + size, :]
                at += size


def project(info, xs, places, ws, terms):
    cols = ws[0].shape[1]
    rows = sum(x.shape[0] for x in xs)
    args = [info, *xs, *ws]
    more = terms is not None
    if more:
        args.append(terms)
    return pl.pallas_call(
        functools.partial(project_kernel, places, more),
        out_shape=jax.ShapeDtypeStruct((NR * NZ, TOK, cols), jnp.bfloat16),
        in_specs=[pl.BlockSpec(memory_space=SMEM)]
        + [pl.BlockSpec(memory_space=VMEM)] * (len(args) - 1),
        out_specs=pl.BlockSpec(memory_space=VMEM),
        scratch_shapes=[VMEM((rows, GROUP * HEAD), jnp.bfloat16)],
        input_output_aliases={len(args) - 1: 0} if more else {},
        compiler_params=pltpu.CompilerParams(vmem_limit_bytes=24 * MIB),
        cost_estimate=pl.CostEstimate(
            flops=2 * rows * 2048 * 2048 * 2, bytes_accessed=12 * MIB, transcendentals=0
        ),
        name="project",
    )(*args)


def ring(x):
    half = x.shape[0] // 2
    up = down = x
    got = []
    for _ in range(3):
        up, down = move(up, z_shift(1)), move(down, z_shift(-1))
        up, down = lax.optimization_barrier((up, down))
        got.append((up, down))
    got.append((move(up[:half], z_shift(1)), move(down[half:], z_shift(-1))))
    return got


def shards(queries, keys, values, out_weight, cache_len, block_order):
    blk = lax.axis_index("blk")
    info = jnp.stack([blk // NR, blk % NR, cache_len[0]]).astype(jnp.int32)
    q0, kv0 = prep(block_order, queries, keys, values)
    around = [
        (at * NR + r, ((at + 1 - 2 * (r % 2)) % NZ) * NR + r)
        for at in range(NZ)
        for r in range(NR)
    ]
    x1 = move(kv0, around)
    kv1 = move(kv0, swap(1))
    q1 = move(q0, swap(1))
    y1 = move(kv1, around)
    q2 = move(q0, swap(2))
    w0 = out_weight
    w2_upper = move(later(w0[:W_CUT], q2), swap(2))

    pair = lambda s: ((s, 0), (s, 1))
    own = ((0, 0),)
    near_q = [q0, q1]
    near = flash(info, [own], [kv0], near_q, None)
    x2 = move(later(x1, near[1]), around)
    y2 = move(y1, around)
    near = flash(info, [pair(1)], [x1, y1], near_q, near)
    x3 = move(later(x2, near[1]), around)
    q3 = move(later(q2, near[1]), swap(1))
    far_q = [q2, q3]
    far = flash(info, [own, pair(1)], [kv0, x1, y1], far_q, None, after=near[1:])
    x4, y3 = move(later(x3, far[1]), around), move(later(y2, far[1]), around)
    w1 = move(later(w0, far[1]), swap(1))
    w2_lower = move(later(w0[W_CUT:], far[1]), swap(2))
    near = flash(info, [pair(2)], [x2, y2], near_q, near, after=[far[1], w2_upper])
    far = flash(info, [pair(2)], [x2, y2], far_q, far, after=near[1:])
    end, last_kv = ((4, 0),), [x3, y3, x4]
    near = flash(info, [pair(3), end], last_kv, near_q, near, last=True, after=far[1:])
    far = flash(info, [pair(3), end], last_kv, far_q, far, last=True, after=[near[1]])
    far_here = merge([far[0], move(far[1], swap(1))], False)
    far_there = move(far_here, swap(2))
    attn = merge([near[0], move(near[1], swap(1)), far_there], True)

    got = ring(attn)
    w3_upper = move(later(w2_upper, far_here), swap(1))
    w3_lower = move(later(w2_lower, far_here), swap(1))
    ws = [w0, w1, w2_upper, w2_lower, w3_upper, w3_lower]
    places = [(0, 0), (-1, 0), (1, 0), (-2, 0), (2, 0)]
    terms = project(info, [attn, *got[0], *got[1]], places, ws, None)
    places = [(-3, 0), (3, 0), (4, 0), (4, TOK // 2)]
    terms = project(info, [*got[2], *got[3]], places, ws, terms)
    groups = [
        [(zz * NR + rr) * 8 + h for rr in range(NR) for h in range(8)] for zz in range(NZ)
    ]
    parts = lax.all_to_all(
        terms, ("blk", "head"), 0, 0, tiled=True, axis_index_groups=groups
    )
    parts = parts.reshape(NR, 8, TOK, parts.shape[-1])
    total = jnp.sum(parts.astype(jnp.float32), axis=1)
    return total.reshape(NR * TOK, -1).astype(jnp.bfloat16)


def solution(mesh):
    return jax.shard_map(
        shards,
        mesh=mesh,
        in_specs=(
            P("blk", "head"),
            P("blk", "head"),
            P("blk", "head"),
            P("head", "blk"),
            P(),
            P("blk"),
        ),
        out_specs=P("head", "blk"),
        check_vma=False,
    )
```

```python
import functools
import math

import jax
import jax.numpy as jnp
from jax import lax
from jax.experimental import pallas as pl
from jax.experimental.pallas import tpu as pltpu
from jax.sharding import PartitionSpec as P

HEAD = 128
GROUP = 16
TOK = 64
ROWS = GROUP * TOK
C_ROWS = 512
SCALE = math.log2(math.e) / math.sqrt(HEAD)
LOW = -1e30
RB = 256
STEP = 1024
NZ, NR = 8, 4
EXT = 32
MIB = 2**20
VMEM = pltpu.VMEM
SMEM = pltpu.SMEM


def z_shift(step):
    return [(z * NR + r, ((z + step) % NZ) * NR + r) for z in range(NZ) for r in range(NR)]


def swap(bit):
    return [(b, b ^ bit) for b in range(NZ * NR)]


def move(x, pairs):
    return lax.ppermute(x, "blk", pairs)


def later(x, event):
    return lax.optimization_barrier((x, event))[0]


def prep_kernel(order_ref, q_ref, k_ref, v_ref, o_ref, kv_ref, sem):
    copies = [
        pltpu.make_async_copy(k_ref, kv_ref.at[:C_ROWS], sem.at[GROUP]),
        pltpu.make_async_copy(v_ref, kv_ref.at[C_ROWS:], sem.at[GROUP + 1]),
    ]
    for g in range(GROUP):
        rows, cols = pl.ds(g * TOK, TOK), pl.ds(g * HEAD, HEAD)
        copies.append(pltpu.make_async_copy(q_ref.at[:, cols], o_ref.at[rows], sem.at[g]))
    for copy in copies:
        copy.start()
    place = jnp.full((16, HEAD), order_ref[0], jnp.int32).astype(jnp.float32)
    o_ref[ROWS : ROWS + 16, :] = place.astype(jnp.bfloat16)
    for copy in copies:
        copy.wait()


def prep(order, queries, keys, values):
    return pl.pallas_call(
        prep_kernel,
        out_shape=[
            jax.ShapeDtypeStruct((ROWS + 16, HEAD), jnp.bfloat16),
            jax.ShapeDtypeStruct((2 * C_ROWS, HEAD), jnp.bfloat16),
        ],
        in_specs=[pl.BlockSpec(memory_space=SMEM)] + [pl.BlockSpec(memory_space=pl.ANY)] * 3,
        out_specs=[pl.BlockSpec(memory_space=VMEM)] * 2,
        scratch_shapes=[pltpu.SemaphoreType.DMA((GROUP + 2,))],
        compiler_params=pltpu.CompilerParams(vmem_limit_bytes=56 * MIB),
        name="prep",
    )(order, queries, keys, values)


def compact(x):
    eye = lax.broadcasted_iota(jnp.int32, (HEAD, HEAD), 0) == lax.broadcasted_iota(
        jnp.int32, (HEAD, HEAD), 1
    )
    return jnp.sum(jnp.where(eye, x, 0.0), axis=0, keepdims=True)


def spread(line):
    return jnp.broadcast_to(line, (HEAD, HEAD)).T


def write_lse(o_ref, lse):
    hi = lse.astype(jnp.bfloat16).astype(jnp.float32)
    mid = (lse - hi).astype(jnp.bfloat16).astype(jnp.float32)
    low = lse - hi - mid
    tail = jnp.concatenate([hi, mid, low, jnp.zeros_like(lse)], axis=0)
    o_ref[ROWS : ROWS + EXT, :] = tail.astype(jnp.bfloat16)


def read_lse(ref):
    tail = ref[ROWS : ROWS + EXT, :].astype(jnp.float32)
    return tail[0:8, :] + tail[8:16, :] + tail[16:24, :]


def pack(o_ref, acc, top, first):
    lines = []
    for j in range(ROWS // HEAD):
        held = slice(first + j * HEAD, first + (j + 1) * HEAD)
        total = acc[held, HEAD:]
        x = acc[held, :HEAD] / total
        o_ref[j * HEAD : (j + 1) * HEAD, :] = x.astype(jnp.bfloat16)
        lines.append(compact(top[held, :] + jnp.log2(total)))
    write_lse(o_ref, jnp.concatenate(lines, axis=0))


def absorb(q, keys, values, into, origin, rows_at, count, first_key, size, pos):
    acc, top = into
    halves = STEP // RB

    def scores(row):
        k = keys[pl.ds(first_key, size), :]
        s = lax.dot_general(
            q[pl.ds(row, RB), :], k, (((1,), (1,)), ((), ())), preferred_element_type=jnp.float32
        )
        s = s * SCALE
        if pos is not None:
            line = lax.broadcasted_iota(jnp.int32, (RB, size), 0) % TOK
            col = lax.broadcasted_iota(jnp.int32, (RB, size), 1)
            s = jnp.where(pos[1] + col <= pos[0] + line, s, LOW)
        return s

    def weigh(row, s):
        new = jnp.max(s, axis=1, keepdims=True)
        shrink = None
        if origin is None:
            new = jnp.broadcast_to(new, (RB, HEAD))
        else:
            old = origin[1][pl.ds(row, RB), :]
            new = jnp.maximum(old, new)
            shrink = jnp.exp2(old - new)
        top[pl.ds(row, RB), :] = new
        p = jnp.exp2(s - jnp.tile(new, (1, size // HEAD))).astype(jnp.bfloat16)
        return p, shrink

    def add(row, p, shrink):
        v1 = values[pl.ds(first_key, size), :]
        more = jnp.dot(p, v1, preferred_element_type=jnp.float32)
        if origin is not None:
            more += origin[0][pl.ds(row, RB), :] * jnp.tile(shrink, (1, 2))
        acc[pl.ds(row, RB), :] = more

    def step(t, carry):
        row = lambda i: pl.multiple_of(rows_at + t * STEP + i * RB, RB)
        s, held = scores(row(0)), None
        for i in range(halves):
            later = scores(row(i + 1)) if i + 1 < halves else None
            p, shrink = weigh(row(i), s)
            if held is not None:
                add(*held)
            held, s = (row(i), p, shrink), later
        add(*held)
        return carry

    lax.fori_loop(0, count, step, 0)


def flash_kernel(blocks, last, n_after, info_ref, *refs):
    n = sum(len(block) for block in blocks)
    n_q = 2
    kv_refs, q_refs, refs = refs[:n], refs[n : n + n_q], refs[n + n_q :]
    fresh = not last and len(refs) == 5 + n_after
    origin = None
    if not fresh:
        origin, refs = refs[:2], refs[2:]
    refs = refs[n_after:]
    if last:
        out_refs, refs = refs[:2], refs[2:]
    acc, top, q, keys, values = refs
    into = (acc, top)
    for j, ref in enumerate(kv_refs):
        rows = slice(j * C_ROWS, (j + 1) * C_ROWS)
        keys[rows, :] = ref[:C_ROWS, :]
        values[rows, :HEAD] = ref[C_ROWS:, :]
    values[:, HEAD:] = jnp.ones((n * C_ROWS, HEAD), jnp.bfloat16)
    z, r, cached = info_ref[0], info_ref[1], info_ref[2]
    way = 1 - 2 * jnp.bitwise_and(r, 1)
    pos = []
    for i, ref in enumerate(q_refs):
        q[i * ROWS : (i + 1) * ROWS, :] = ref[:ROWS, :]
        place = jnp.max(ref[ROWS : ROWS + 16, :].astype(jnp.float32)).astype(jnp.int32)
        pos.append(cached + TOK * place)

    def base_of(piece):
        return (
            lax.rem(z + NZ - piece[0] * way, NZ) * NR + jnp.bitwise_xor(r, piece[1])
        ) * C_ROWS

    at = 0
    for b, block in enumerate(blocks):
        start = into if b else origin
        first_key = at * C_ROWS
        bases = [base_of(piece) for piece in block]
        end = functools.reduce(jnp.maximum, bases) + C_ROWS - 1
        seen = end <= functools.reduce(jnp.minimum, pos)

        @pl.when(seen)
        def _():
            whole = len(block) * C_ROWS
            steps = n_q * ROWS // STEP
            absorb(q, keys, values, into, start, 0, steps, first_key, whole, None)

        @pl.when(jnp.logical_not(seen))
        def _():
            if start is None:
                acc[...] = jnp.zeros(acc.shape, jnp.float32)
                top[...] = jnp.full(top.shape, LOW, jnp.float32)
            elif start is not into:
                acc[...] = start[0][...]
                top[...] = start[1][...]

            def one(j, carry):
                i, piece = j % 2, j // 2
                first = jnp.where(i == 0, pos[0], pos[1])
                base = bases[0] if len(block) == 1 else jnp.where(piece == 0, *bases)
                key = pl.multiple_of(first_key + piece * C_ROWS, C_ROWS)

                @pl.when(base <= first + TOK - 1)
                def _():
                    steps = ROWS // STEP
                    where = (first, base)
                    absorb(q, keys, values, into, into, i * ROWS, steps, key, C_ROWS, where)

                return carry

            lax.fori_loop(0, n_q * len(block), one, 0)

        at += len(block)

    if last:
        for i in range(n_q):
            pack(out_refs[i], acc, top, i * ROWS)


def flash(info, blocks, kvs, queries, state, last=False, after=(), weight=16):
    n = len(kvs)
    whole = pl.BlockSpec(memory_space=VMEM)
    args = [info, *kvs, *queries]
    aliases = {}
    if state is not None:
        if not last:
            aliases = {len(args): 0, len(args) + 1: 1}
        args += list(state)
    in_specs = [pl.BlockSpec(memory_space=SMEM)] + [whole] * (len(args) - 1)
    args += list(after)
    in_specs += [pl.BlockSpec(memory_space=pl.ANY)] * len(after)
    scratch = [
        VMEM((2 * ROWS, HEAD), jnp.bfloat16),
        VMEM((n * C_ROWS, HEAD), jnp.bfloat16),
        VMEM((n * C_ROWS, 2 * HEAD), jnp.bfloat16),
    ]
    if last:
        out_shape = [jax.ShapeDtypeStruct((ROWS + EXT, HEAD), jnp.bfloat16)] * 2
        scratch = [
            VMEM((2 * ROWS, 2 * HEAD), jnp.float32),
            VMEM((2 * ROWS, HEAD), jnp.float32),
        ] + scratch
    else:
        out_shape = [
            jax.ShapeDtypeStruct((2 * ROWS, 2 * HEAD), jnp.float32),
            jax.ShapeDtypeStruct((2 * ROWS, HEAD), jnp.float32),
        ]
    return pl.pallas_call(
        functools.partial(flash_kernel, blocks, last, len(after)),
        out_shape=out_shape,
        in_specs=in_specs,
        out_specs=[whole] * 2,
        scratch_shapes=scratch,
        input_output_aliases=aliases,
        compiler_params=pltpu.CompilerParams(vmem_limit_bytes=24 * MIB),
        cost_estimate=pl.CostEstimate(
            flops=2 * ROWS * n * C_ROWS * HEAD * weight, bytes_accessed=weight * MIB // 4, transcendentals=0
        ),
        name="flash",
    )(*args)


def merge_kernel(final, *refs):
    parts, o_ref = refs[:-1], refs[-1]
    lses = [read_lse(ref) for ref in parts]
    top = functools.reduce(jnp.maximum, lses)
    weights = [jnp.exp2(lse - top) for lse in lses]
    total = functools.reduce(jnp.add, weights)
    shares = [weight / total for weight in weights]
    for j in range(ROWS // HEAD):
        rows = slice(j * HEAD, (j + 1) * HEAD)
        x = jnp.zeros((HEAD, HEAD), jnp.float32)
        for share, ref in zip(shares, parts):
            x += spread(share[j : j + 1, :]) * ref[rows, :].astype(jnp.float32)
        x = x.astype(jnp.bfloat16)
        if final:
            for g in range(2):
                cols = (2 * j + g) * HEAD
                o_ref[:, cols : cols + HEAD] = x[g * TOK : (g + 1) * TOK, :]
        else:
            o_ref[rows, :] = x
    if not final:
        write_lse(o_ref, top + jnp.log2(total))


def merge(parts, final):
    shape = (TOK, GROUP * HEAD) if final else (ROWS + EXT, HEAD)
    return pl.pallas_call(
        functools.partial(merge_kernel, final),
        out_shape=jax.ShapeDtypeStruct(shape, jnp.bfloat16),
        in_specs=[pl.BlockSpec(memory_space=VMEM)] * len(parts),
        out_specs=pl.BlockSpec(memory_space=VMEM),
        compiler_params=pltpu.CompilerParams(vmem_limit_bytes=8 * MIB),
        name="merge",
    )(*parts)


W_CUT = 1280


def project_kernel(places, more, info_ref, *refs):
    n = len(places)
    x_refs, w_refs, refs = refs[: n], refs[n : n + 6], refs[n + 6 :]
    o_ref, held = refs[-2], refs[-1]
    z, r = info_ref[0], info_ref[1]
    if more:
        o_ref[...] = refs[0][...]
    at = 0
    for x in x_refs:
        held[at : at + x.shape[0], :] = x[...]
        at += x.shape[0]
    for i in range(NR):
        piece = jnp.bitwise_xor(r, i)
        for c in range(0, 512, 256):
            cols = slice(c, c + 256)
            if i < 2:
                y = jnp.dot(held[...], w_refs[i][:, cols], preferred_element_type=jnp.float32)
            else:
                upper, lower = w_refs[2 * i - 2], w_refs[2 * i - 1]
                y = jnp.dot(
                    held[:, :W_CUT], upper[:, cols], preferred_element_type=jnp.float32
                ) + jnp.dot(
                    held[:, W_CUT:], lower[:, cols], preferred_element_type=jnp.float32
                )
            y = y.astype(jnp.bfloat16)
            at = 0
            for place, start, x in [(p, s, x) for (p, s), x in zip(places, x_refs)]:
                size = x.shape[0]
                owner = lax.rem(z + NZ + place, NZ)
                o_ref[piece * NZ + owner, start : start + size, cols] = y[at : at + size, :]
                at += size


def project(info, xs, places, ws, terms):
    cols = ws[0].shape[1]
    rows = sum(x.shape[0] for x in xs)
    args = [info, *xs, *ws]
    more = terms is not None
    if more:
        args.append(terms)
    return pl.pallas_call(
        functools.partial(project_kernel, places, more),
        out_shape=jax.ShapeDtypeStruct((NR * NZ, TOK, cols), jnp.bfloat16),
        in_specs=[pl.BlockSpec(memory_space=SMEM)]
        + [pl.BlockSpec(memory_space=VMEM)] * (len(args) - 1),
        out_specs=pl.BlockSpec(memory_space=VMEM),
        scratch_shapes=[VMEM((rows, GROUP * HEAD), jnp.bfloat16)],
        input_output_aliases={len(args) - 1: 0} if more else {},
        compiler_params=pltpu.CompilerParams(vmem_limit_bytes=24 * MIB),
        cost_estimate=pl.CostEstimate(
            flops=2 * rows * 2048 * 2048 * 2, bytes_accessed=12 * MIB, transcendentals=0
        ),
        name="project",
    )(*args)


def ring(x):
    half = x.shape[0] // 2
    up = down = x
    got = []
    for _ in range(3):
        up, down = move(up, z_shift(1)), move(down, z_shift(-1))
        up, down = lax.optimization_barrier((up, down))
        got.append((up, down))
    got.append((move(up[:half], z_shift(1)), move(down[half:], z_shift(-1))))
    return got


def shards(queries, keys, values, out_weight, cache_len, block_order):
    blk = lax.axis_index("blk")
    info = jnp.stack([blk // NR, blk % NR, cache_len[0]]).astype(jnp.int32)
    q0, kv0 = prep(block_order, queries, keys, values)
    around = [
        (at * NR + r, ((at + 1 - 2 * (r % 2)) % NZ) * NR + r)
        for at in range(NZ)
        for r in range(NR)
    ]
    x1 = move(kv0, around)
    kv1 = move(kv0, swap(1))
    q1 = move(q0, swap(1))
    y1 = move(kv1, around)
    q2 = move(q0, swap(2))
    w0 = out_weight
    w2_upper = move(later(w0[:W_CUT], q2), swap(2))

    pair = lambda s: ((s, 0), (s, 1))
    own = ((0, 0),)
    near_q = [q0, q1]
    near = flash(info, [own], [kv0], near_q, None, weight=1)
    x2 = move(later(x1, near[1]), around)
    y2 = move(y1, around)
    near = flash(info, [pair(1)], [x1, y1], near_q, near, weight=1)
    x3 = move(later(x2, near[1]), around)
    q3 = move(later(q2, near[1]), swap(1))
    far_q = [q2, q3]
    far = flash(info, [own, pair(1)], [kv0, x1, y1], far_q, None, after=near[1:])
    x4, y3 = move(later(x3, far[1]), around), move(later(y2, far[1]), around)
    near = flash(info, [pair(2)], [x2, y2], near_q, near, after=far[1:])
    far = flash(info, [pair(2)], [x2, y2], far_q, far, after=near[1:])
    end, last_kv = ((4, 0),), [x3, y3, x4]
    near = flash(info, [pair(3), end], last_kv, near_q, near, last=True, after=far[1:])
    far = flash(info, [pair(3), end], last_kv, far_q, far, last=True, after=[near[1], w2_upper])
    far_here = merge([far[0], move(far[1], swap(1))], False)
    far_there = move(far_here, swap(2))
    w1 = move(later(w0, far_here), swap(1))
    w3_upper = move(later(w2_upper, far_here), swap(1))
    attn = merge([later(near[0], (w1, w3_upper)), move(near[1], swap(1)), far_there], True)

    got = ring(attn)
    w2_lower = move(later(w0[W_CUT:], far_there), swap(2))
    w3_lower = move(later(w2_lower, got[2]), swap(1))
    ws = [w0, w1, w2_upper, w2_lower, w3_upper, w3_lower]
    places = [(0, 0), (-1, 0), (1, 0), (-2, 0), (2, 0)]
    terms = project(info, [attn, *got[0], *got[1]], places, ws, None)
    places = [(-3, 0), (3, 0), (4, 0), (4, TOK // 2)]
    terms = project(info, [*got[2], *got[3]], places, ws, terms)
    groups = [
        [(zz * NR + rr) * 8 + h for rr in range(NR) for h in range(8)] for zz in range(NZ)
    ]
    parts = lax.all_to_all(
        terms, ("blk", "head"), 0, 0, tiled=True, axis_index_groups=groups
    )
    parts = parts.reshape(NR, 8, TOK, parts.shape[-1])
    total = jnp.sum(parts.astype(jnp.float32), axis=1)
    return total.reshape(NR * TOK, -1).astype(jnp.bfloat16)


def solution(mesh):
    return jax.shard_map(
        shards,
        mesh=mesh,
        in_specs=(
            P("blk", "head"),
            P("blk", "head"),
            P("blk", "head"),
            P("head", "blk"),
            P(),
            P("blk"),
        ),
        out_specs=P("head", "blk"),
        check_vma=False,
    )
```

```python
import functools
import math

import jax
import jax.numpy as jnp
from jax import lax
from jax.experimental import pallas as pl
from jax.experimental.pallas import tpu as pltpu
from jax.sharding import PartitionSpec as P

HEAD = 128
GROUP = 16
TOK = 64
ROWS = GROUP * TOK
C_ROWS = 512
SCALE = math.log2(math.e) / math.sqrt(HEAD)
LOW = -1e30
RB = 256
STEP = 1024
NZ, NR = 8, 4
EXT = 32
MIB = 2**20
VMEM = pltpu.VMEM
SMEM = pltpu.SMEM


def z_shift(step):
    return [(z * NR + r, ((z + step) % NZ) * NR + r) for z in range(NZ) for r in range(NR)]


def swap(bit):
    return [(b, b ^ bit) for b in range(NZ * NR)]


def move(x, pairs):
    return lax.ppermute(x, "blk", pairs)


def later(x, event):
    return lax.optimization_barrier((x, event))[0]


def prep_kernel(order_ref, q_ref, k_ref, v_ref, o_ref, kv_ref, sem):
    copies = [
        pltpu.make_async_copy(k_ref, kv_ref.at[:C_ROWS], sem.at[GROUP]),
        pltpu.make_async_copy(v_ref, kv_ref.at[C_ROWS:], sem.at[GROUP + 1]),
    ]
    for g in range(GROUP):
        rows, cols = pl.ds(g * TOK, TOK), pl.ds(g * HEAD, HEAD)
        copies.append(pltpu.make_async_copy(q_ref.at[:, cols], o_ref.at[rows], sem.at[g]))
    for copy in copies:
        copy.start()
    place = jnp.full((16, HEAD), order_ref[0], jnp.int32).astype(jnp.float32)
    o_ref[ROWS : ROWS + 16, :] = place.astype(jnp.bfloat16)
    for copy in copies:
        copy.wait()


def prep(order, queries, keys, values):
    return pl.pallas_call(
        prep_kernel,
        out_shape=[
            jax.ShapeDtypeStruct((ROWS + 16, HEAD), jnp.bfloat16),
            jax.ShapeDtypeStruct((2 * C_ROWS, HEAD), jnp.bfloat16),
        ],
        in_specs=[pl.BlockSpec(memory_space=SMEM)] + [pl.BlockSpec(memory_space=pl.ANY)] * 3,
        out_specs=[pl.BlockSpec(memory_space=VMEM)] * 2,
        scratch_shapes=[pltpu.SemaphoreType.DMA((GROUP + 2,))],
        compiler_params=pltpu.CompilerParams(vmem_limit_bytes=56 * MIB),
        name="prep",
    )(order, queries, keys, values)


def compact(x):
    eye = lax.broadcasted_iota(jnp.int32, (HEAD, HEAD), 0) == lax.broadcasted_iota(
        jnp.int32, (HEAD, HEAD), 1
    )
    return jnp.sum(jnp.where(eye, x, 0.0), axis=0, keepdims=True)


def spread(line):
    return jnp.broadcast_to(line, (HEAD, HEAD)).T


def write_lse(o_ref, lse):
    hi = lse.astype(jnp.bfloat16).astype(jnp.float32)
    mid = (lse - hi).astype(jnp.bfloat16).astype(jnp.float32)
    low = lse - hi - mid
    tail = jnp.concatenate([hi, mid, low, jnp.zeros_like(lse)], axis=0)
    o_ref[ROWS : ROWS + EXT, :] = tail.astype(jnp.bfloat16)


def read_lse(ref):
    tail = ref[ROWS : ROWS + EXT, :].astype(jnp.float32)
    return tail[0:8, :] + tail[8:16, :] + tail[16:24, :]


def pack(o_ref, acc, top, first):
    lines = []
    for j in range(ROWS // HEAD):
        held = slice(first + j * HEAD, first + (j + 1) * HEAD)
        total = acc[held, HEAD:]
        x = acc[held, :HEAD] / total
        o_ref[j * HEAD : (j + 1) * HEAD, :] = x.astype(jnp.bfloat16)
        lines.append(compact(top[held, :] + jnp.log2(total)))
    write_lse(o_ref, jnp.concatenate(lines, axis=0))


def absorb(q, keys, values, into, origin, rows_at, count, first_key, size, pos):
    acc, top = into
    halves = STEP // RB

    def scores(row):
        k = keys[pl.ds(first_key, size), :]
        s = lax.dot_general(
            q[pl.ds(row, RB), :], k, (((1,), (1,)), ((), ())), preferred_element_type=jnp.float32
        )
        s = s * SCALE
        if pos is not None:
            line = lax.broadcasted_iota(jnp.int32, (RB, size), 0) % TOK
            col = lax.broadcasted_iota(jnp.int32, (RB, size), 1)
            s = jnp.where(pos[1] + col <= pos[0] + line, s, LOW)
        return s

    def weigh(row, s):
        new = jnp.max(s, axis=1, keepdims=True)
        shrink = None
        if origin is None:
            new = jnp.broadcast_to(new, (RB, HEAD))
        else:
            old = origin[1][pl.ds(row, RB), :]
            new = jnp.maximum(old, new)
            shrink = jnp.exp2(old - new)
        top[pl.ds(row, RB), :] = new
        p = jnp.exp2(s - jnp.tile(new, (1, size // HEAD))).astype(jnp.bfloat16)
        return p, shrink

    def add(row, p, shrink):
        v1 = values[pl.ds(first_key, size), :]
        more = jnp.dot(p, v1, preferred_element_type=jnp.float32)
        if origin is not None:
            more += origin[0][pl.ds(row, RB), :] * jnp.tile(shrink, (1, 2))
        acc[pl.ds(row, RB), :] = more

    def step(t, carry):
        row = lambda i: pl.multiple_of(rows_at + t * STEP + i * RB, RB)
        s, held = scores(row(0)), None
        for i in range(halves):
            later = scores(row(i + 1)) if i + 1 < halves else None
            p, shrink = weigh(row(i), s)
            if held is not None:
                add(*held)
            held, s = (row(i), p, shrink), later
        add(*held)
        return carry

    lax.fori_loop(0, count, step, 0)


def flash_kernel(blocks, last, n_after, info_ref, *refs):
    n = sum(len(block) for block in blocks)
    n_q = 2
    kv_refs, q_refs, refs = refs[:n], refs[n : n + n_q], refs[n + n_q :]
    fresh = not last and len(refs) == 5 + n_after
    origin = None
    if not fresh:
        origin, refs = refs[:2], refs[2:]
    refs = refs[n_after:]
    if last:
        out_refs, refs = refs[:2], refs[2:]
    acc, top, q, keys, values = refs
    into = (acc, top)
    for j, ref in enumerate(kv_refs):
        rows = slice(j * C_ROWS, (j + 1) * C_ROWS)
        keys[rows, :] = ref[:C_ROWS, :]
        values[rows, :HEAD] = ref[C_ROWS:, :]
    values[:, HEAD:] = jnp.ones((n * C_ROWS, HEAD), jnp.bfloat16)
    z, r, cached = info_ref[0], info_ref[1], info_ref[2]
    way = 1 - 2 * jnp.bitwise_and(r, 1)
    pos = []
    for i, ref in enumerate(q_refs):
        q[i * ROWS : (i + 1) * ROWS, :] = ref[:ROWS, :]
        place = jnp.max(ref[ROWS : ROWS + 16, :].astype(jnp.float32)).astype(jnp.int32)
        pos.append(cached + TOK * place)

    def base_of(piece):
        return (
            lax.rem(z + NZ - piece[0] * way, NZ) * NR + jnp.bitwise_xor(r, piece[1])
        ) * C_ROWS

    at = 0
    for b, block in enumerate(blocks):
        start = into if b else origin
        first_key = at * C_ROWS
        bases = [base_of(piece) for piece in block]
        end = functools.reduce(jnp.maximum, bases) + C_ROWS - 1
        seen = end <= functools.reduce(jnp.minimum, pos)

        @pl.when(seen)
        def _():
            whole = len(block) * C_ROWS
            steps = n_q * ROWS // STEP
            absorb(q, keys, values, into, start, 0, steps, first_key, whole, None)

        @pl.when(jnp.logical_not(seen))
        def _():
            if start is None:
                acc[...] = jnp.zeros(acc.shape, jnp.float32)
                top[...] = jnp.full(top.shape, LOW, jnp.float32)
            elif start is not into:
                acc[...] = start[0][...]
                top[...] = start[1][...]

            def one(j, carry):
                i, piece = j % 2, j // 2
                first = jnp.where(i == 0, pos[0], pos[1])
                base = bases[0] if len(block) == 1 else jnp.where(piece == 0, *bases)
                key = pl.multiple_of(first_key + piece * C_ROWS, C_ROWS)

                @pl.when(base <= first + TOK - 1)
                def _():
                    steps = ROWS // STEP
                    where = (first, base)
                    absorb(q, keys, values, into, into, i * ROWS, steps, key, C_ROWS, where)

                return carry

            lax.fori_loop(0, n_q * len(block), one, 0)

        at += len(block)

    if last:
        for i in range(n_q):
            pack(out_refs[i], acc, top, i * ROWS)


def flash(info, blocks, kvs, queries, state, last=False, after=(), weight=16):
    n = len(kvs)
    whole = pl.BlockSpec(memory_space=VMEM)
    args = [info, *kvs, *queries]
    aliases = {}
    if state is not None:
        if not last:
            aliases = {len(args): 0, len(args) + 1: 1}
        args += list(state)
    in_specs = [pl.BlockSpec(memory_space=SMEM)] + [whole] * (len(args) - 1)
    args += list(after)
    in_specs += [pl.BlockSpec(memory_space=pl.ANY)] * len(after)
    scratch = [
        VMEM((2 * ROWS, HEAD), jnp.bfloat16),
        VMEM((n * C_ROWS, HEAD), jnp.bfloat16),
        VMEM((n * C_ROWS, 2 * HEAD), jnp.bfloat16),
    ]
    if last:
        out_shape = [jax.ShapeDtypeStruct((ROWS + EXT, HEAD), jnp.bfloat16)] * 2
        scratch = [
            VMEM((2 * ROWS, 2 * HEAD), jnp.float32),
            VMEM((2 * ROWS, HEAD), jnp.float32),
        ] + scratch
    else:
        out_shape = [
            jax.ShapeDtypeStruct((2 * ROWS, 2 * HEAD), jnp.float32),
            jax.ShapeDtypeStruct((2 * ROWS, HEAD), jnp.float32),
        ]
    return pl.pallas_call(
        functools.partial(flash_kernel, blocks, last, len(after)),
        out_shape=out_shape,
        in_specs=in_specs,
        out_specs=[whole] * 2,
        scratch_shapes=scratch,
        input_output_aliases=aliases,
        compiler_params=pltpu.CompilerParams(vmem_limit_bytes=24 * MIB),
        cost_estimate=pl.CostEstimate(
            flops=2 * ROWS * n * C_ROWS * HEAD * weight, bytes_accessed=weight * MIB // 4, transcendentals=0
        ),
        name="flash",
    )(*args)


def merge_kernel(final, *refs):
    parts, o_ref = refs[:-1], refs[-1]
    lses = [read_lse(ref) for ref in parts]
    top = functools.reduce(jnp.maximum, lses)
    weights = [jnp.exp2(lse - top) for lse in lses]
    total = functools.reduce(jnp.add, weights)
    shares = [weight / total for weight in weights]
    for j in range(ROWS // HEAD):
        rows = slice(j * HEAD, (j + 1) * HEAD)
        x = jnp.zeros((HEAD, HEAD), jnp.float32)
        for share, ref in zip(shares, parts):
            x += spread(share[j : j + 1, :]) * ref[rows, :].astype(jnp.float32)
        x = x.astype(jnp.bfloat16)
        if final:
            for g in range(2):
                cols = (2 * j + g) * HEAD
                o_ref[:, cols : cols + HEAD] = x[g * TOK : (g + 1) * TOK, :]
        else:
            o_ref[rows, :] = x
    if not final:
        write_lse(o_ref, top + jnp.log2(total))


def merge(parts, final):
    shape = (TOK, GROUP * HEAD) if final else (ROWS + EXT, HEAD)
    return pl.pallas_call(
        functools.partial(merge_kernel, final),
        out_shape=jax.ShapeDtypeStruct(shape, jnp.bfloat16),
        in_specs=[pl.BlockSpec(memory_space=VMEM)] * len(parts),
        out_specs=pl.BlockSpec(memory_space=VMEM),
        compiler_params=pltpu.CompilerParams(vmem_limit_bytes=8 * MIB),
        name="merge",
    )(*parts)


W_CUT = 1280


def project_kernel(places, more, info_ref, *refs):
    n = len(places)
    x_refs, w_refs, refs = refs[: n], refs[n : n + 6], refs[n + 6 :]
    o_ref, held = refs[-2], refs[-1]
    z, r = info_ref[0], info_ref[1]
    if more:
        o_ref[...] = refs[0][...]
    at = 0
    for x in x_refs:
        held[at : at + x.shape[0], :] = x[...]
        at += x.shape[0]
    for i in range(NR):
        piece = jnp.bitwise_xor(r, i)
        for c in range(0, 512, 256):
            cols = slice(c, c + 256)
            if i < 2:
                y = jnp.dot(held[...], w_refs[i][:, cols], preferred_element_type=jnp.float32)
            else:
                upper, lower = w_refs[2 * i - 2], w_refs[2 * i - 1]
                y = jnp.dot(
                    held[:, :W_CUT], upper[:, cols], preferred_element_type=jnp.float32
                ) + jnp.dot(
                    held[:, W_CUT:], lower[:, cols], preferred_element_type=jnp.float32
                )
            y = y.astype(jnp.bfloat16)
            at = 0
            for place, start, x in [(p, s, x) for (p, s), x in zip(places, x_refs)]:
                size = x.shape[0]
                owner = lax.rem(z + NZ + place, NZ)
                o_ref[piece * NZ + owner, start : start + size, cols] = y[at : at + size, :]
                at += size


def project(info, xs, places, ws, terms):
    cols = ws[0].shape[1]
    rows = sum(x.shape[0] for x in xs)
    args = [info, *xs, *ws]
    more = terms is not None
    if more:
        args.append(terms)
    return pl.pallas_call(
        functools.partial(project_kernel, places, more),
        out_shape=jax.ShapeDtypeStruct((NR * NZ, TOK, cols), jnp.bfloat16),
        in_specs=[pl.BlockSpec(memory_space=SMEM)]
        + [pl.BlockSpec(memory_space=VMEM)] * (len(args) - 1),
        out_specs=pl.BlockSpec(memory_space=VMEM),
        scratch_shapes=[VMEM((rows, GROUP * HEAD), jnp.bfloat16)],
        input_output_aliases={len(args) - 1: 0} if more else {},
        compiler_params=pltpu.CompilerParams(vmem_limit_bytes=24 * MIB),
        cost_estimate=pl.CostEstimate(
            flops=2 * rows * 2048 * 2048 * 2, bytes_accessed=12 * MIB, transcendentals=0
        ),
        name="project",
    )(*args)


def ring(x):
    half = x.shape[0] // 2
    up = down = x
    got = []
    for _ in range(3):
        up, down = move(up, z_shift(1)), move(down, z_shift(-1))
        up, down = lax.optimization_barrier((up, down))
        got.append((up, down))
    got.append((move(up[:half], z_shift(1)), move(down[half:], z_shift(-1))))
    return got


def shards(queries, keys, values, out_weight, cache_len, block_order):
    blk = lax.axis_index("blk")
    info = jnp.stack([blk // NR, blk % NR, cache_len[0]]).astype(jnp.int32)
    q0, kv0 = prep(block_order, queries, keys, values)
    around = [
        (at * NR + r, ((at + 1 - 2 * (r % 2)) % NZ) * NR + r)
        for at in range(NZ)
        for r in range(NR)
    ]
    x1 = move(kv0, around)
    kv1 = move(kv0, swap(1))
    q1 = move(q0, swap(1))
    y1 = move(kv1, around)
    q2 = move(q0, swap(2))
    w0 = out_weight
    w2_upper = move(later(w0[:W_CUT], q2), swap(2))

    pair = lambda s: ((s, 0), (s, 1))
    own = ((0, 0),)
    near_q = [q0, q1]
    near = flash(info, [own], [kv0], near_q, None, weight=1)
    x2, y2 = move(later(x1, y1), around), move(y1, around)
    q3 = move(later(q2, near[1]), swap(1))
    near = flash(info, [pair(1)], [x1, y1], near_q, near, after=[x2, q3], weight=1)
    x3 = move(x2, around)
    far_q = [q2, q3]
    far = flash(info, [own, pair(1)], [kv0, x1, y1], far_q, None, after=near[1:])
    x4, y3 = move(later(x3, far[1]), around), move(later(y2, far[1]), around)
    near = flash(info, [pair(2)], [x2, y2], near_q, near, after=[far[1], x3])
    far = flash(info, [pair(2)], [x2, y2], far_q, far, after=near[1:])
    end, last_kv = ((4, 0),), [x3, y3, x4]
    near = flash(info, [pair(3), end], last_kv, near_q, near, last=True, after=far[1:])
    far = flash(info, [pair(3), end], last_kv, far_q, far, last=True, after=[near[1], w2_upper])
    far_here = merge([far[0], move(far[1], swap(1))], False)
    far_there = move(far_here, swap(2))
    w1 = move(later(w0, far_here), swap(1))
    w3_upper = move(later(w2_upper, far_here), swap(1))
    attn = merge([later(near[0], (w1, w3_upper)), move(near[1], swap(1)), far_there], True)

    got = ring(attn)
    w2_lower = move(later(w0[W_CUT:], far_there), swap(2))
    w3_lower = move(later(w2_lower, got[2]), swap(1))
    ws = [w0, w1, w2_upper, w2_lower, w3_upper, w3_lower]
    places = [(0, 0), (-1, 0), (1, 0), (-2, 0), (2, 0)]
    terms = project(info, [attn, *got[0], *got[1]], places, ws, None)
    places = [(-3, 0), (3, 0), (4, 0), (4, TOK // 2)]
    terms = project(info, [*got[2], *got[3]], places, ws, terms)
    groups = [
        [(zz * NR + rr) * 8 + h for rr in range(NR) for h in range(8)] for zz in range(NZ)
    ]
    parts = lax.all_to_all(
        terms, ("blk", "head"), 0, 0, tiled=True, axis_index_groups=groups
    )
    parts = parts.reshape(NR, 8, TOK, parts.shape[-1])
    total = jnp.sum(parts.astype(jnp.float32), axis=1)
    return total.reshape(NR * TOK, -1).astype(jnp.bfloat16)


def solution(mesh):
    return jax.shard_map(
        shards,
        mesh=mesh,
        in_specs=(
            P("blk", "head"),
            P("blk", "head"),
            P("blk", "head"),
            P("head", "blk"),
            P(),
            P("blk"),
        ),
        out_specs=P("head", "blk"),
        check_vma=False,
    )
```

```python
import functools
import math

import jax
import jax.numpy as jnp
from jax import lax
from jax.experimental import pallas as pl
from jax.experimental.pallas import tpu as pltpu
from jax.sharding import PartitionSpec as P

HEAD = 128
GROUP = 16
TOK = 64
ROWS = GROUP * TOK
C_ROWS = 512
SCALE = math.log2(math.e) / math.sqrt(HEAD)
LOW = -1e30
RB = 512
STEP = 1024
NZ, NR = 8, 4
EXT = 32
MIB = 2**20
VMEM = pltpu.VMEM
SMEM = pltpu.SMEM


def z_shift(step):
    return [(z * NR + r, ((z + step) % NZ) * NR + r) for z in range(NZ) for r in range(NR)]


def swap(bit):
    return [(b, b ^ bit) for b in range(NZ * NR)]


def move(x, pairs):
    return lax.ppermute(x, "blk", pairs)


def later(x, event):
    return lax.optimization_barrier((x, event))[0]


def prep_kernel(order_ref, q_ref, k_ref, v_ref, o_ref, kv_ref, sem):
    copies = [
        pltpu.make_async_copy(k_ref, kv_ref.at[:C_ROWS], sem.at[GROUP]),
        pltpu.make_async_copy(v_ref, kv_ref.at[C_ROWS:], sem.at[GROUP + 1]),
    ]
    for g in range(GROUP):
        rows, cols = pl.ds(g * TOK, TOK), pl.ds(g * HEAD, HEAD)
        copies.append(pltpu.make_async_copy(q_ref.at[:, cols], o_ref.at[rows], sem.at[g]))
    for copy in copies:
        copy.start()
    place = jnp.full((16, HEAD), order_ref[0], jnp.int32).astype(jnp.float32)
    o_ref[ROWS : ROWS + 16, :] = place.astype(jnp.bfloat16)
    for copy in copies:
        copy.wait()


def prep(order, queries, keys, values):
    return pl.pallas_call(
        prep_kernel,
        out_shape=[
            jax.ShapeDtypeStruct((ROWS + 16, HEAD), jnp.bfloat16),
            jax.ShapeDtypeStruct((2 * C_ROWS, HEAD), jnp.bfloat16),
        ],
        in_specs=[pl.BlockSpec(memory_space=SMEM)] + [pl.BlockSpec(memory_space=pl.ANY)] * 3,
        out_specs=[pl.BlockSpec(memory_space=VMEM)] * 2,
        scratch_shapes=[pltpu.SemaphoreType.DMA((GROUP + 2,))],
        compiler_params=pltpu.CompilerParams(vmem_limit_bytes=56 * MIB),
        name="prep",
    )(order, queries, keys, values)


def compact(x):
    eye = lax.broadcasted_iota(jnp.int32, (HEAD, HEAD), 0) == lax.broadcasted_iota(
        jnp.int32, (HEAD, HEAD), 1
    )
    return jnp.sum(jnp.where(eye, x, 0.0), axis=0, keepdims=True)


def spread(line):
    return jnp.broadcast_to(line, (HEAD, HEAD)).T


def write_lse(o_ref, lse):
    hi = lse.astype(jnp.bfloat16).astype(jnp.float32)
    mid = (lse - hi).astype(jnp.bfloat16).astype(jnp.float32)
    low = lse - hi - mid
    tail = jnp.concatenate([hi, mid, low, jnp.zeros_like(lse)], axis=0)
    o_ref[ROWS : ROWS + EXT, :] = tail.astype(jnp.bfloat16)


def read_lse(ref):
    tail = ref[ROWS : ROWS + EXT, :].astype(jnp.float32)
    return tail[0:8, :] + tail[8:16, :] + tail[16:24, :]


def pack(o_ref, acc, top, first):
    lines = []
    for j in range(ROWS // HEAD):
        held = slice(first + j * HEAD, first + (j + 1) * HEAD)
        total = acc[held, HEAD:]
        x = acc[held, :HEAD] / total
        o_ref[j * HEAD : (j + 1) * HEAD, :] = x.astype(jnp.bfloat16)
        lines.append(compact(top[held, :] + jnp.log2(total)))
    write_lse(o_ref, jnp.concatenate(lines, axis=0))


def absorb(q, keys, values, into, origin, rows_at, count, first_key, size, pos):
    acc, top = into
    halves = STEP // RB

    def scores(row):
        k = keys[pl.ds(first_key, size), :]
        s = lax.dot_general(
            q[pl.ds(row, RB), :], k, (((1,), (1,)), ((), ())), preferred_element_type=jnp.float32
        )
        s = s * SCALE
        if pos is not None:
            line = lax.broadcasted_iota(jnp.int32, (RB, size), 0) % TOK
            col = lax.broadcasted_iota(jnp.int32, (RB, size), 1)
            s = jnp.where(pos[1] + col <= pos[0] + line, s, LOW)
        return s

    def weigh(row, s):
        new = jnp.max(s, axis=1, keepdims=True)
        shrink = None
        if origin is None:
            new = jnp.broadcast_to(new, (RB, HEAD))
        else:
            old = origin[1][pl.ds(row, RB), :]
            new = jnp.maximum(old, new)
            shrink = jnp.exp2(old - new)
        top[pl.ds(row, RB), :] = new
        p = jnp.exp2(s - jnp.tile(new, (1, size // HEAD))).astype(jnp.bfloat16)
        return p, shrink

    def add(row, p, shrink):
        v1 = values[pl.ds(first_key, size), :]
        more = jnp.dot(p, v1, preferred_element_type=jnp.float32)
        if origin is not None:
            more += origin[0][pl.ds(row, RB), :] * jnp.tile(shrink, (1, 2))
        acc[pl.ds(row, RB), :] = more

    def step(t, carry):
        row = lambda i: pl.multiple_of(rows_at + t * STEP + i * RB, RB)
        s, held = scores(row(0)), None
        for i in range(halves):
            later = scores(row(i + 1)) if i + 1 < halves else None
            p, shrink = weigh(row(i), s)
            if held is not None:
                add(*held)
            held, s = (row(i), p, shrink), later
        add(*held)
        return carry

    lax.fori_loop(0, count, step, 0)


def flash_kernel(blocks, last, n_after, info_ref, *refs):
    n = sum(len(block) for block in blocks)
    n_q = 2
    kv_refs, q_refs, refs = refs[:n], refs[n : n + n_q], refs[n + n_q :]
    fresh = not last and len(refs) == 5 + n_after
    origin = None
    if not fresh:
        origin, refs = refs[:2], refs[2:]
    refs = refs[n_after:]
    if last:
        out_refs, refs = refs[:2], refs[2:]
    acc, top, q, keys, values = refs
    into = (acc, top)
    for j, ref in enumerate(kv_refs):
        rows = slice(j * C_ROWS, (j + 1) * C_ROWS)
        keys[rows, :] = ref[:C_ROWS, :]
        values[rows, :HEAD] = ref[C_ROWS:, :]
    values[:, HEAD:] = jnp.ones((n * C_ROWS, HEAD), jnp.bfloat16)
    z, r, cached = info_ref[0], info_ref[1], info_ref[2]
    way = 1 - 2 * jnp.bitwise_and(r, 1)
    pos = []
    for i, ref in enumerate(q_refs):
        q[i * ROWS : (i + 1) * ROWS, :] = ref[:ROWS, :]
        place = jnp.max(ref[ROWS : ROWS + 16, :].astype(jnp.float32)).astype(jnp.int32)
        pos.append(cached + TOK * place)

    def base_of(piece):
        return (
            lax.rem(z + NZ - piece[0] * way, NZ) * NR + jnp.bitwise_xor(r, piece[1])
        ) * C_ROWS

    at = 0
    for b, block in enumerate(blocks):
        start = into if b else origin
        first_key = at * C_ROWS
        bases = [base_of(piece) for piece in block]
        end = functools.reduce(jnp.maximum, bases) + C_ROWS - 1
        seen = end <= functools.reduce(jnp.minimum, pos)

        @pl.when(seen)
        def _():
            whole = len(block) * C_ROWS
            steps = n_q * ROWS // STEP
            absorb(q, keys, values, into, start, 0, steps, first_key, whole, None)

        @pl.when(jnp.logical_not(seen))
        def _():
            if start is None:
                acc[...] = jnp.zeros(acc.shape, jnp.float32)
                top[...] = jnp.full(top.shape, LOW, jnp.float32)
            elif start is not into:
                acc[...] = start[0][...]
                top[...] = start[1][...]

            def one(j, carry):
                i, piece = j % 2, j // 2
                first = jnp.where(i == 0, pos[0], pos[1])
                base = bases[0] if len(block) == 1 else jnp.where(piece == 0, *bases)
                key = pl.multiple_of(first_key + piece * C_ROWS, C_ROWS)

                @pl.when(base <= first + TOK - 1)
                def _():
                    steps = ROWS // STEP
                    where = (first, base)
                    absorb(q, keys, values, into, into, i * ROWS, steps, key, C_ROWS, where)

                return carry

            lax.fori_loop(0, n_q * len(block), one, 0)

        at += len(block)

    if last:
        for i in range(n_q):
            pack(out_refs[i], acc, top, i * ROWS)


def flash(info, blocks, kvs, queries, state, last=False, after=(), weight=16):
    n = len(kvs)
    whole = pl.BlockSpec(memory_space=VMEM)
    args = [info, *kvs, *queries]
    aliases = {}
    if state is not None:
        if not last:
            aliases = {len(args): 0, len(args) + 1: 1}
        args += list(state)
    in_specs = [pl.BlockSpec(memory_space=SMEM)] + [whole] * (len(args) - 1)
    args += list(after)
    in_specs += [pl.BlockSpec(memory_space=pl.ANY)] * len(after)
    scratch = [
        VMEM((2 * ROWS, HEAD), jnp.bfloat16),
        VMEM((n * C_ROWS, HEAD), jnp.bfloat16),
        VMEM((n * C_ROWS, 2 * HEAD), jnp.bfloat16),
    ]
    if last:
        out_shape = [jax.ShapeDtypeStruct((ROWS + EXT, HEAD), jnp.bfloat16)] * 2
        scratch = [
            VMEM((2 * ROWS, 2 * HEAD), jnp.float32),
            VMEM((2 * ROWS, HEAD), jnp.float32),
        ] + scratch
    else:
        out_shape = [
            jax.ShapeDtypeStruct((2 * ROWS, 2 * HEAD), jnp.float32),
            jax.ShapeDtypeStruct((2 * ROWS, HEAD), jnp.float32),
        ]
    return pl.pallas_call(
        functools.partial(flash_kernel, blocks, last, len(after)),
        out_shape=out_shape,
        in_specs=in_specs,
        out_specs=[whole] * 2,
        scratch_shapes=scratch,
        input_output_aliases=aliases,
        compiler_params=pltpu.CompilerParams(vmem_limit_bytes=24 * MIB),
        cost_estimate=pl.CostEstimate(
            flops=2 * ROWS * n * C_ROWS * HEAD * weight, bytes_accessed=weight * MIB // 4, transcendentals=0
        ),
        name="flash",
    )(*args)


def merge_kernel(final, *refs):
    parts, o_ref = refs[:-1], refs[-1]
    lses = [read_lse(ref) for ref in parts]
    top = functools.reduce(jnp.maximum, lses)
    weights = [jnp.exp2(lse - top) for lse in lses]
    total = functools.reduce(jnp.add, weights)
    shares = [weight / total for weight in weights]
    for j in range(ROWS // HEAD):
        rows = slice(j * HEAD, (j + 1) * HEAD)
        x = jnp.zeros((HEAD, HEAD), jnp.float32)
        for share, ref in zip(shares, parts):
            x += spread(share[j : j + 1, :]) * ref[rows, :].astype(jnp.float32)
        x = x.astype(jnp.bfloat16)
        if final:
            for g in range(2):
                cols = (2 * j + g) * HEAD
                o_ref[:, cols : cols + HEAD] = x[g * TOK : (g + 1) * TOK, :]
        else:
            o_ref[rows, :] = x
    if not final:
        write_lse(o_ref, top + jnp.log2(total))


def merge(parts, final):
    shape = (TOK, GROUP * HEAD) if final else (ROWS + EXT, HEAD)
    return pl.pallas_call(
        functools.partial(merge_kernel, final),
        out_shape=jax.ShapeDtypeStruct(shape, jnp.bfloat16),
        in_specs=[pl.BlockSpec(memory_space=VMEM)] * len(parts),
        out_specs=pl.BlockSpec(memory_space=VMEM),
        compiler_params=pltpu.CompilerParams(vmem_limit_bytes=8 * MIB),
        name="merge",
    )(*parts)


W_CUT = 1280


def project_kernel(places, more, info_ref, *refs):
    n = len(places)
    x_refs, w_refs, refs = refs[: n], refs[n : n + 6], refs[n + 6 :]
    o_ref, held = refs[-2], refs[-1]
    z, r = info_ref[0], info_ref[1]
    if more:
        o_ref[...] = refs[0][...]
    at = 0
    for x in x_refs:
        held[at : at + x.shape[0], :] = x[...]
        at += x.shape[0]
    for i in range(NR):
        piece = jnp.bitwise_xor(r, i)
        for c in range(0, 512, 256):
            cols = slice(c, c + 256)
            if i < 2:
                y = jnp.dot(held[...], w_refs[i][:, cols], preferred_element_type=jnp.float32)
            else:
                upper, lower = w_refs[2 * i - 2], w_refs[2 * i - 1]
                y = jnp.dot(
                    held[:, :W_CUT], upper[:, cols], preferred_element_type=jnp.float32
                ) + jnp.dot(
                    held[:, W_CUT:], lower[:, cols], preferred_element_type=jnp.float32
                )
            y = y.astype(jnp.bfloat16)
            at = 0
            for place, start, x in [(p, s, x) for (p, s), x in zip(places, x_refs)]:
                size = x.shape[0]
                owner = lax.rem(z + NZ + place, NZ)
                o_ref[piece * NZ + owner, start : start + size, cols] = y[at : at + size, :]
                at += size


def project(info, xs, places, ws, terms):
    cols = ws[0].shape[1]
    rows = sum(x.shape[0] for x in xs)
    args = [info, *xs, *ws]
    more = terms is not None
    if more:
        args.append(terms)
    return pl.pallas_call(
        functools.partial(project_kernel, places, more),
        out_shape=jax.ShapeDtypeStruct((NR * NZ, TOK, cols), jnp.bfloat16),
        in_specs=[pl.BlockSpec(memory_space=SMEM)]
        + [pl.BlockSpec(memory_space=VMEM)] * (len(args) - 1),
        out_specs=pl.BlockSpec(memory_space=VMEM),
        scratch_shapes=[VMEM((rows, GROUP * HEAD), jnp.bfloat16)],
        input_output_aliases={len(args) - 1: 0} if more else {},
        compiler_params=pltpu.CompilerParams(vmem_limit_bytes=24 * MIB),
        cost_estimate=pl.CostEstimate(
            flops=2 * rows * 2048 * 2048 * 2, bytes_accessed=12 * MIB, transcendentals=0
        ),
        name="project",
    )(*args)


def ring(x):
    half = x.shape[0] // 2
    up = down = x
    got = []
    for _ in range(3):
        up, down = move(up, z_shift(1)), move(down, z_shift(-1))
        up, down = lax.optimization_barrier((up, down))
        got.append((up, down))
    got.append((move(up[:half], z_shift(1)), move(down[half:], z_shift(-1))))
    return got


def shards(queries, keys, values, out_weight, cache_len, block_order):
    blk = lax.axis_index("blk")
    info = jnp.stack([blk // NR, blk % NR, cache_len[0]]).astype(jnp.int32)
    q0, kv0 = prep(block_order, queries, keys, values)
    around = [
        (at * NR + r, ((at + 1 - 2 * (r % 2)) % NZ) * NR + r)
        for at in range(NZ)
        for r in range(NR)
    ]
    x1 = move(kv0, around)
    kv1 = move(kv0, swap(1))
    q1 = move(q0, swap(1))
    y1 = move(kv1, around)
    q2 = move(q0, swap(2))
    w0 = out_weight
    w2_upper = move(later(w0[:W_CUT], q2), swap(2))

    pair = lambda s: ((s, 0), (s, 1))
    own = ((0, 0),)
    near_q = [q0, q1]
    near = flash(info, [own], [kv0], near_q, None, weight=1)
    x2, y2 = move(later(x1, y1), around), move(y1, around)
    q3 = move(later(q2, near[1]), swap(1))
    near = flash(info, [pair(1)], [x1, y1], near_q, near, after=[x2, q3], weight=1)
    x3 = move(x2, around)
    far_q = [q2, q3]
    far = flash(info, [own, pair(1)], [kv0, x1, y1], far_q, None, after=near[1:])
    x4, y3 = move(later(x3, far[1]), around), move(later(y2, far[1]), around)
    near = flash(info, [pair(2)], [x2, y2], near_q, near, after=[far[1], x3])
    far = flash(info, [pair(2)], [x2, y2], far_q, far, after=near[1:])
    end, last_kv = ((4, 0),), [x3, y3, x4]
    near = flash(info, [pair(3), end], last_kv, near_q, near, last=True, after=far[1:])
    far = flash(info, [pair(3), end], last_kv, far_q, far, last=True, after=[near[1], w2_upper])
    far_here = merge([far[0], move(far[1], swap(1))], False)
    far_there = move(far_here, swap(2))
    w1 = move(later(w0, far_here), swap(1))
    w3_upper = move(later(w2_upper, far_here), swap(1))
    attn = merge([later(near[0], (w1, w3_upper)), move(near[1], swap(1)), far_there], True)

    got = ring(attn)
    w2_lower = move(later(w0[W_CUT:], far_there), swap(2))
    w3_lower = move(later(w2_lower, got[2]), swap(1))
    ws = [w0, w1, w2_upper, w2_lower, w3_upper, w3_lower]
    places = [(0, 0), (-1, 0), (1, 0), (-2, 0), (2, 0)]
    terms = project(info, [attn, *got[0], *got[1]], places, ws, None)
    places = [(-3, 0), (3, 0), (4, 0), (4, TOK // 2)]
    terms = project(info, [*got[2], *got[3]], places, ws, terms)
    groups = [
        [(zz * NR + rr) * 8 + h for rr in range(NR) for h in range(8)] for zz in range(NZ)
    ]
    parts = lax.all_to_all(
        terms, ("blk", "head"), 0, 0, tiled=True, axis_index_groups=groups
    )
    parts = parts.reshape(NR, 8, TOK, parts.shape[-1])
    total = jnp.sum(parts.astype(jnp.float32), axis=1)
    return total.reshape(NR * TOK, -1).astype(jnp.bfloat16)


def solution(mesh):
    return jax.shard_map(
        shards,
        mesh=mesh,
        in_specs=(
            P("blk", "head"),
            P("blk", "head"),
            P("blk", "head"),
            P("head", "blk"),
            P(),
            P("blk"),
        ),
        out_specs=P("head", "blk"),
        check_vma=False,
    )
```
